512 devices in a mesh: shape: 16 (over z_lo, x), query: 32 (over z_hi, y, core).
Axes of the slice: x: 4, y: 4, z: 16 (z_hi: 4, z_lo: 4; z = z_hi * 4 + z_lo), core: 2. Of those that a mesh axis runs over, the one named last changes fastest.
Arguments:
- queries: bfloat16 [16, 4096, 512], P('shape', 'query'), may hold values from -128 to 128
- keys: bfloat16 [16, 1024, 512], P('shape', 'query'), may hold values from -5 to 5
- values: bfloat16 [16, 1024, 512], P('shape', 'query'), may hold values from -6 to 6
- out_weight: bfloat16 [512, 512], replicated, may hold values from -0.25 to 0.25
- out_grad: float32 [16, 4096, 512], P('shape', 'query'), may hold values from -6 to 6
Outputs:
- query_grad: float32 [16, 4096, 512], P('shape', 'query')
- key_grad: float32 [16, 1024, 512], P('shape', 'query')
- value_grad: float32 [16, 1024, 512], P('shape', 'query')
- weight_grad: float32 [512, 512], replicated
The draws below stay inside these ranges and needn't reach their ends.
All inputs are finite; a program needn't handle non-finite values.
Results may differ from the reference program's by a relative error of at most 0.02.
Values may be sent and summed in bfloat16 or wider, within the bound.
A program may use at most 64 MiB of HBM per device.

```python
import math
import jax
import jax.numpy as jnp
from jax import lax

D = 512
HEADS = 8
HEAD = 64
M = 1024
SHAPES = 16
POINTS = 4096


def draw_keys(key, part):
    base = jax.random.normal(jax.random.fold_in(key, 11), (SHAPES, M, D), jnp.float32)
    base = jnp.clip(base, -5.0, 5.0)
    return base.astype(jnp.bfloat16)


def draw_queries(key, part):
    base = jax.random.normal(jax.random.fold_in(key, 23), (SHAPES, POINTS, D), jnp.float32)
    base = jnp.clip(base, -6.0, 6.0)
    return jnp.clip(base, -128.0, 128.0).astype(jnp.bfloat16)


def level_of(rng, extent, split, smallest, largest):
    def one(dim, parts):
        draws = jax.random.uniform(jax.random.fold_in(jax.random.fold_in(rng, 6), dim), (parts,), jnp.float32, smallest / len(split), largest / len(split))
        return jnp.repeat(jnp.exp(draws), extent[dim] // parts).reshape((-1,) + (1,) * (len(extent) - dim - 1))

    gain = one(*split[0])
    for cut in split[1:]:
        gain = gain * one(*cut)
    return gain


def scatter_about(own_key, shape, deviation, most, cuts=(), held_as=jnp.bfloat16):
    result = jax.random.normal(own_key, shape, jnp.float32) * deviation
    if len(cuts) > 0:
        result = level_of(own_key, shape, cuts, -0.22, 0.18) * result
    return jnp.clip(result, min=-most, max=most).astype(held_as)


def setup_inputs(seed: int = 0) -> dict:
    streams_of = jax.random.split(jax.random.key(seed), 6)
    return {
        "queries": draw_queries(jax.random.fold_in(streams_of[5], 71), 0),
        "keys": draw_keys(jax.random.fold_in(streams_of[5], 71), 0),
        "values": scatter_about(streams_of[2], (SHAPES, M, D), 1.0, 6.0, ((0, 16), (1, 32))),
        "out_weight": scatter_about(streams_of[3], (D, D), D ** -0.5, 0.25),
        "out_grad": scatter_about(streams_of[4], (SHAPES, POINTS, D), 1.0, 6.0, ((0, 16), (1, 32)), jnp.float32),
    }


def one_shape(items, out_weight):
    query_rows, key_rows, value_rows, grad_rows = items
    scale = 1.0 / math.sqrt(HEAD)
    grad_b = grad_rows.astype(jnp.bfloat16)
    d_attn = jnp.dot(grad_b, out_weight.T, preferred_element_type=jnp.float32).astype(jnp.bfloat16)
    q_list, k_list, v_list, a_list = ([], [], [], [])
    for head_index in range(HEADS):
        cols = slice(head_index * HEAD, (head_index + 1) * HEAD)
        qh = query_rows[:, cols]
        kh = key_rows[:, cols]
        vh = value_rows[:, cols]
        scores = jnp.dot(qh, kh.T, preferred_element_type=jnp.float32) * scale
        top = lax.optimization_barrier(jnp.max(scores, axis=1, keepdims=True))
        lse = top + jnp.log(lax.optimization_barrier(jnp.sum(jnp.exp(scores - top), axis=1, keepdims=True)))
        probs = jnp.exp(scores - lse)
        probs_b = probs.astype(jnp.bfloat16)
        attn_h = jnp.dot(probs_b, vh, preferred_element_type=jnp.float32).astype(jnp.bfloat16)
        dh = d_attn[:, cols]
        delta = lax.optimization_barrier(jnp.sum(dh.astype(jnp.float32) * attn_h.astype(jnp.float32), axis=1, keepdims=True))
        d_probs = jnp.dot(dh, vh.T, preferred_element_type=jnp.float32)
        d_scores = (probs * (d_probs - delta) * scale).astype(jnp.bfloat16)
        q_list.append(jnp.dot(d_scores, kh, preferred_element_type=jnp.float32))
        k_list.append(jnp.dot(d_scores.T, qh, preferred_element_type=jnp.float32))
        v_list.append(jnp.dot(probs_b.T, dh, preferred_element_type=jnp.float32))
        a_list.append(attn_h)
    attn = jnp.concatenate(a_list, axis=1)
    weight_term = jnp.dot(attn.T, grad_b, preferred_element_type=jnp.float32)
    return (jnp.concatenate(q_list, axis=1), jnp.concatenate(k_list, axis=1), jnp.concatenate(v_list, axis=1), weight_term)

def reference(queries, keys, values, out_weight, out_grad):
    results = lax.map(lambda items: one_shape(items, out_weight), (queries, keys, values, out_grad))
    query_grad, key_grad, value_grad, terms = results
    weight_grad = lax.optimization_barrier(jnp.sum(terms, axis=0)) * (1.0 / SHAPES)
    return (query_grad, key_grad, value_grad, weight_grad)
```

```python
import math

import jax
import jax.numpy as jnp
from jax import lax
from jax.experimental import pallas as pl
from jax.experimental.pallas import tpu as pltpu
from jax.sharding import PartitionSpec as P

MESH = pl.DeviceIdType.MESH
BF = jnp.bfloat16
F32 = jnp.float32

ROWS = 128
LAT = 32
D = 512
HALF = 256
SHAPES = 16
SCALE = 1.0 / math.sqrt(64)
LOG2E = 1.4426950408889634


def nt(a, b):
    return lax.dot_general(a, b, (((1,), (1,)), ((), ())), preferred_element_type=F32)


def tn(a, b):
    return lax.dot_general(a, b, (((0,), (0,)), ((), ())), preferred_element_type=F32)


def nn(a, b):
    return lax.dot_general(a, b, (((1,), (0,)), ((), ())), preferred_element_type=F32)


def kernel(
    q_hbm, k_hbm, v_hbm, w_hbm, g_hbm,
    dq_out, dk_out, dv_out, dw_out,
    kv, q2, gb, gst, w_v, dat, da, s_ref, pb_ref, ds_ref, at, qbd, dbd, qst, dst,
    dkv, ry, rz, red, fin, dqs, wpart, w_a, w_b_src, w_b, w_c,
    loc, sib_s, sib_r, ag_s, ag_r, ry_s, ry_r, rz_s, rz_r, fin_s, fin_r, dq_s, dq_r,
    a_s, a_r, b_s, b_r, c_s, c_r, d_s, d_r, e_s, e_r,
):
    shape_at = lax.axis_index("shape")
    query_at = lax.axis_index("query")
    core = lax.rem(query_at, 2)
    other = 1 - core
    y = lax.rem(lax.div(query_at, 2), 4)
    zh = lax.div(query_at, 8)
    x = lax.rem(shape_at, 4)
    zl = lax.div(shape_at, 4)
    y1, y2, y3 = [lax.rem(y + i, 4) for i in (1, 2, 3)]
    z1, z2, z3 = [lax.rem(zh + i, 4) for i in (1, 2, 3)]
    sib = (shape_at, query_at + 1 - 2 * core)
    to_z = {1: (shape_at, z1 * 8 + y * 2 + core), -1: (shape_at, z3 * 8 + y * 2 + core)}
    to_y = {1: (shape_at, zh * 8 + y1 * 2 + core), -1: (shape_at, zh * 8 + y3 * 2 + core)}
    plane = x * 4 + y
    line = zh * 4 + zl

    def plane_peer(i):
        return (zl * 4 + lax.div(i, 4), zh * 8 + lax.rem(i, 4) * 2 + core)

    def line_peer(i):
        return (lax.rem(i, 4) * 4 + x, lax.div(i, 4) * 8 + y * 2 + core)

    barrier = pltpu.get_barrier_semaphore()
    pl.semaphore_signal(barrier, inc=1, device_id=sib, device_id_type=MESH)

    @pl.loop(1, 16)
    def _(i):
        pl.semaphore_signal(barrier, inc=1, device_id=line_peer(lax.rem(line + i, 16)), device_id_type=MESH)
        pl.semaphore_signal(barrier, inc=1, device_id=plane_peer(lax.rem(plane + i, 16)), device_id_type=MESH)

    mine = pl.ds(pl.multiple_of(core * HALF, HALF), HALF)
    theirs = pl.ds(pl.multiple_of(other * HALF, HALF), HALF)
    my_rows = pl.ds(pl.multiple_of(core * ROWS, ROWS), ROWS)

    def block_cols(c, b):
        return pl.ds(pl.multiple_of(c * HALF + b * 128, 128), 128)

    local = [pltpu.make_async_copy(g_hbm, gst, loc.at[0])]
    for b in range(2):
        for t, ref in enumerate((k_hbm, v_hbm)):
            local.append(
                pltpu.make_async_copy(ref.at[:, block_cols(core, b)], kv.at[b, zh, y, core, t], loc.at[1 + 2 * b + t])
            )
    local.append(pltpu.make_async_copy(w_hbm.at[mine, :], w_v, loc.at[5]))
    local.append(pltpu.make_async_copy(q_hbm.at[:, mine], q2.at[my_rows, :], loc.at[6]))
    for c in local:
        c.start()
    local[0].wait()
    gb[my_rows, :] = gst[...].astype(BF)

    sends = []

    def send(src, dst, ss, rs, dev):
        c = pltpu.make_async_remote_copy(
            src_ref=src, dst_ref=dst, send_sem=ss, recv_sem=rs, device_id=dev, device_id_type=MESH
        )
        c.start()
        sends.append(c)

    def got(ref, ss, rs):
        pltpu.make_async_remote_copy(
            src_ref=ref, dst_ref=ref, send_sem=ss, recv_sem=rs, device_id=sib, device_id_type=MESH
        ).wait_recv()

    pl.semaphore_wait(barrier, 31)

    for b in range(2):
        for t, ref in enumerate((k_hbm, v_hbm)):
            send(ref.at[:, block_cols(other, b)], kv.at[b, zh, y, core, t], sib_s.at[2 * b + t], sib_r.at[2 * b + t], sib)
    send(gb.at[my_rows, :], gb.at[my_rows, :], sib_s.at[4], sib_r.at[4], sib)
    send(q_hbm.at[:, theirs], q2.at[my_rows, :], sib_s.at[5], sib_r.at[5], sib)

    def sub(z, yy, c):
        return kv.at[:, z, yy, c]

    def piece(z, yy):
        return kv.at[:, z, yy]

    def ag_send(ref, z, yy, c, slot, dev):
        send(ref, ref, ag_s.at[z, yy, c, slot], ag_r.at[z, yy, c], dev)

    def ag_got(ref, z, yy, c):
        got(ref, ag_s.at[z, yy, c, 0], ag_r.at[z, yy, c])

    for c in local[1:5]:
        c.wait()
    for c in (core, other):
        if c is other:
            for b in range(2):
                for t in range(2):
                    got(kv.at[b, zh, y, other, t], sib_s.at[2 * b + t], sib_r.at[2 * b + t])
        ag_send(sub(zh, y, c), zh, y, c, 0, to_z[1])
        ag_send(sub(zh, y, c), zh, y, c, 1, to_z[-1])
        ag_send(sub(zh, y, c), zh, y, c, 2, to_y[1])
        ag_send(sub(zh, y, c), zh, y, c, 3, to_y[-1])
    for c in local[5:]:
        c.wait()
    got(gb.at[pl.ds(pl.multiple_of(other * ROWS, ROWS), ROWS), :], sib_s.at[4], sib_r.at[4])
    got(q2.at[pl.ds(pl.multiple_of(other * ROWS, ROWS), ROWS), :], sib_s.at[5], sib_r.at[5])

    ag_got(sub(z3, y, 0), z3, y, 0)
    ag_send(sub(z3, y, 0), z3, y, 0, 0, to_z[1])
    ag_got(sub(z1, y, 1), z1, y, 1)
    ag_send(sub(z1, y, 1), z1, y, 1, 1, to_z[-1])
    ag_got(sub(z3, y, 1), z3, y, 1)
    ag_send(piece(z3, y), z3, y, 0, 2, to_y[1])
    ag_send(piece(z3, y), z3, y, 0, 3, to_y[-1])
    ag_got(sub(z1, y, 0), z1, y, 0)
    ag_send(piece(z1, y), z1, y, 0, 2, to_y[1])
    ag_send(piece(z1, y), z1, y, 0, 3, to_y[-1])
    ag_got(sub(zh, y3, 0), zh, y3, 0)
    ag_send(sub(zh, y3, 0), zh, y3, 0, 2, to_y[1])
    ag_got(sub(zh, y1, 1), zh, y1, 1)
    ag_send(sub(zh, y1, 1), zh, y1, 1, 3, to_y[-1])

    dat[...] = nt(w_v[...], gb[...]).astype(BF)
    da[...] = nt(gb[...], w_v[...]).astype(BF)

    ag_got(sub(z2, y, 0), z2, y, 0)
    ag_got(sub(z2, y, 1), z2, y, 1)
    ag_send(piece(z2, y), z2, y, 0, 2, to_y[1])
    ag_send(piece(z2, y), z2, y, 0, 3, to_y[-1])
    for z in (z3, z1, z2):
        ag_got(piece(z, y3), z, y3, 0)
        ag_send(sub(z, y3, 0), z, y3, 0, 2, to_y[1])
        ag_got(piece(z, y1), z, y1, 0)
        ag_send(sub(z, y1, 1), z, y1, 1, 3, to_y[-1])
    ag_got(sub(zh, y3, 1), zh, y3, 1)
    ag_got(sub(zh, y1, 0), zh, y1, 0)
    for z in (zh, z3, z1, z2):
        for c in range(2):
            ag_got(sub(z, y2, c), z, y2, c)

    def keys_of(b, z):
        return kv[b, z, :, :, 0].reshape(256, 128)

    def values_of(b, z):
        return kv[b, z, :, :, 1].reshape(256, 128)

    def all_of(b, t):
        return kv[b, :, :, :, t].reshape(1024, 128)

    low = lax.broadcasted_iota(jnp.int32, (256, 128), 1) < 64
    zero = jnp.zeros((64, 256), BF)

    def forward(b):
        cols = slice(b * 128, b * 128 + 128)
        q_t = q2[:, cols].T
        qbd[0:64, 0:256] = q_t[0:64]
        qbd[0:64, 256:512] = zero
        qbd[64:128, 0:256] = zero
        qbd[64:128, 256:512] = q_t[64:128]
        top = None
        for r in range(4):
            s = nn(keys_of(b, r), qbd[...])
            s_ref[b, r] = s
            m = jnp.max(s, axis=0, keepdims=True)
            top = m if top is None else jnp.maximum(top, m)
        total = None
        for r in range(4):
            e = jnp.exp2((s_ref[b, r] - top) * (SCALE * LOG2E))
            s_ref[b, r] = e
            m = jnp.sum(e, axis=0, keepdims=True)
            total = m if total is None else total + m
        inv = 1.0 / total
        for r in range(4):
            p = s_ref[b, r] * inv
            s_ref[b, r] = p
            pb_ref[b, r * 256 : r * 256 + 256] = p.astype(BF)
        a = tn(all_of(b, 1), pb_ref[b])
        at[b * 128 : b * 128 + 64, :] = a[0:64, 0:256].astype(BF)
        at[b * 128 + 64 : b * 128 + 128, :] = a[64:128, 256:512].astype(BF)

    def backward(b):
        cols = slice(b * 128, b * 128 + 128)
        prod = dat[cols, :].astype(F32) * at[cols, :].astype(F32)
        delta = jnp.concatenate(
            [jnp.sum(prod[0:64], axis=0, keepdims=True), jnp.sum(prod[64:128], axis=0, keepdims=True)], axis=1
        )
        dbd[0:64, 0:256] = dat[b * 128 : b * 128 + 64, :]
        dbd[0:64, 256:512] = zero
        dbd[64:128, 0:256] = zero
        dbd[64:128, 256:512] = dat[b * 128 + 64 : b * 128 + 128, :]
        none = jnp.zeros((256, 128), BF)
        qst[0:256] = jnp.where(low, q2[:, cols], none)
        qst[256:512] = jnp.where(low, none, q2[:, cols])
        dst[0:256] = jnp.where(low, da[:, cols], none)
        dst[256:512] = jnp.where(low, none, da[:, cols])
        for r in range(4):
            dp = nn(values_of(b, r), dbd[...])
            ds = (s_ref[b, r] * (dp - delta)).astype(BF)
            ds_ref[r * 256 : r * 256 + 256] = ds
            dkv[b, r, :, :, 0] = (nn(ds, qst[...]) * SCALE).astype(BF).reshape(4, 2, LAT, 128)
            dkv[b, r, :, :, 1] = nn(pb_ref[b, r * 256 : r * 256 + 256], dst[...]).astype(BF).reshape(4, 2, LAT, 128)

    def query_part(b):
        a = tn(all_of(b, 0), ds_ref[...]) * SCALE
        for c in range(2):
            rows = slice(c * 128, c * 128 + 128)
            dqs[b, c] = jnp.concatenate([a[0:64, rows], a[64:128, 256 + c * 128 : 384 + c * 128]], axis=0).T
        dq_out[:, block_cols(core, b)] = dqs[b, core]
        send(dqs.at[b, other], dq_out.at[:, block_cols(core, b)], dq_s.at[b], dq_r.at[b], sib)

    def rs_y_start(b):
        send(dkv.at[b, :, y2, 0], ry.at[b, 0, 0], ry_s.at[b, 0, 0], ry_r.at[b, 0, 0], to_y[1])
        send(dkv.at[b, :, y2, 1], ry.at[b, 1, 0], ry_s.at[b, 1, 0], ry_r.at[b, 1, 0], to_y[-1])
        send(dkv.at[b, :, y1, 1], ry.at[b, 0, 1], ry_s.at[b, 0, 1], ry_r.at[b, 0, 1], to_y[1])
        send(dkv.at[b, :, y3, 0], ry.at[b, 1, 1], ry_s.at[b, 1, 1], ry_r.at[b, 1, 1], to_y[-1])

    def add(*parts):
        out = parts[0].astype(F32)
        for p in parts[1:]:
            out = out + p.astype(F32)
        return out

    def rs_y_middle(b):
        got(ry.at[b, 0, 0], ry_s.at[b, 0, 0], ry_r.at[b, 0, 0])
        dkv[b, :, y1, 0] = add(dkv[b, :, y1, 0], ry[b, 0, 0]).astype(BF)
        send(dkv.at[b, :, y1, 0], ry.at[b, 0, 2], ry_s.at[b, 0, 2], ry_r.at[b, 0, 2], to_y[1])
        got(ry.at[b, 1, 0], ry_s.at[b, 1, 0], ry_r.at[b, 1, 0])
        dkv[b, :, y3, 1] = add(dkv[b, :, y3, 1], ry[b, 1, 0]).astype(BF)
        send(dkv.at[b, :, y3, 1], ry.at[b, 1, 2], ry_s.at[b, 1, 2], ry_r.at[b, 1, 2], to_y[-1])

    def rs_z_start(b):
        for i in range(2):
            for k in (1, 2):
                got(ry.at[b, i, k], ry_s.at[b, i, k], ry_r.at[b, i, k])
        red[b, :, 0] = add(dkv[b, :, y, 0], ry[b, 0, 2], ry[b, 1, 1]).astype(BF)
        red[b, :, 1] = add(dkv[b, :, y, 1], ry[b, 0, 1], ry[b, 1, 2]).astype(BF)
        send(red.at[b, z2, 0], rz.at[b, 0, 0], rz_s.at[b, 0, 0], rz_r.at[b, 0, 0], to_z[1])
        send(red.at[b, z2, 1], rz.at[b, 1, 0], rz_s.at[b, 1, 0], rz_r.at[b, 1, 0], to_z[-1])
        send(red.at[b, z1, 1], rz.at[b, 0, 1], rz_s.at[b, 0, 1], rz_r.at[b, 0, 1], to_z[1])
        send(red.at[b, z3, 0], rz.at[b, 1, 1], rz_s.at[b, 1, 1], rz_r.at[b, 1, 1], to_z[-1])

    def rs_z_middle(b):
        got(rz.at[b, 0, 0], rz_s.at[b, 0, 0], rz_r.at[b, 0, 0])
        red[b, z1, 0] = add(red[b, z1, 0], rz[b, 0, 0]).astype(BF)
        send(red.at[b, z1, 0], rz.at[b, 0, 2], rz_s.at[b, 0, 2], rz_r.at[b, 0, 2], to_z[1])
        got(rz.at[b, 1, 0], rz_s.at[b, 1, 0], rz_r.at[b, 1, 0])
        red[b, z3, 1] = add(red[b, z3, 1], rz[b, 1, 0]).astype(BF)
        send(red.at[b, z3, 1], rz.at[b, 1, 2], rz_s.at[b, 1, 2], rz_r.at[b, 1, 2], to_z[-1])

    def rs_end(b):
        for i in range(2):
            for k in (1, 2):
                got(rz.at[b, i, k], rz_s.at[b, i, k], rz_r.at[b, i, k])
        fin[b, 0] = add(red[b, zh, 0], rz[b, 0, 2], rz[b, 1, 1])
        fin[b, 1] = add(red[b, zh, 1], rz[b, 0, 1], rz[b, 1, 2])
        for t, out in enumerate((dk_out, dv_out)):
            send(fin.at[b, other, t], out.at[:, block_cols(core, b)], fin_s.at[b, t], fin_r.at[b, t], sib)
            out[:, block_cols(core, b)] = fin[b, core, t]

    def fin_got(b):
        for t, out in enumerate((dk_out, dv_out)):
            got(out.at[:, block_cols(other, b)], fin_s.at[b, t], fin_r.at[b, t])
        got(dq_out.at[:, block_cols(other, b)], dq_s.at[b], dq_r.at[b])

    def loop_copies(make, how):
        @pl.loop(1, 16)
        def _(i):
            c = make(i)
            getattr(c, how)()

    def remote(src, dst, ss, rs, dev):
        return pltpu.make_async_remote_copy(
            src_ref=src, dst_ref=dst, send_sem=ss, recv_sem=rs, device_id=dev, device_id_type=MESH
        )

    def a_copy(i):
        peer = lax.rem(plane + i, 16)
        return remote(wpart.at[peer], w_a.at[plane], a_s.at[peer], a_r.at[plane], plane_peer(peer))

    def a_in(i):
        return remote(w_a.at[i], w_a.at[i], a_s.at[i], a_r.at[i], sib)

    def b_copy(i):
        peer = lax.rem(line + i, 16)
        return remote(w_b_src.at[lax.rem(peer, 4)], w_b.at[line], b_s.at[peer], b_r.at[line], line_peer(peer))

    def b_in(i):
        return remote(w_b.at[i], w_b.at[i], b_s.at[i], b_r.at[i], sib)

    def d_copy(i):
        peer = lax.rem(plane + i, 16)
        return remote(dw_out.at[core, plane], dw_out.at[core, plane], d_s.at[peer], d_r.at[plane], plane_peer(peer))

    def d_in(i):
        return remote(dw_out.at[core, i], dw_out.at[core, i], d_s.at[i], d_r.at[i], sib)

    def w_start():
        wpart[...] = nn(at[...], gb[...]).astype(BF).reshape(16, 16, D)
        w_a[plane] = wpart[plane]
        loop_copies(a_copy, "start")

    def w_line():
        loop_copies(lambda i: a_in(lax.rem(plane + i, 16)), "wait_recv")
        total = jnp.sum(w_a[...].astype(F32), axis=0)
        for p in range(4):
            w_b_src[p] = total[:, p * 128 : p * 128 + 128].astype(BF)
        w_b[line] = w_b_src[zl]
        loop_copies(b_copy, "start")

    def w_near():
        loop_copies(lambda i: b_in(lax.rem(line + i, 16)), "wait_recv")
        w_c[zl] = (jnp.sum(w_b[...].astype(F32), axis=0) * (1.0 / SHAPES)).astype(BF)
        for k in (1, 2, 3):
            peer = lax.rem(zl + k, 4)
            send(w_c.at[zl], w_c.at[zl], c_s.at[peer], c_r.at[zl], line_peer(zh * 4 + peer))

    def w_plane():
        for k in (1, 2, 3):
            peer = lax.rem(zl + k, 4)
            got(w_c.at[peer], c_s.at[peer], c_r.at[peer])
        for p in range(4):
            dw_out[core, plane, :, p * 128 : p * 128 + 128] = w_c[p]
        loop_copies(d_copy, "start")

    def w_pair():
        loop_copies(lambda i: d_in(lax.rem(plane + i, 16)), "wait_recv")
        send(dw_out.at[core], dw_out.at[core], e_s, e_r, sib)

    def w_end():
        got(dw_out.at[other], e_s, e_r)
        loop_copies(a_copy, "wait_send")
        loop_copies(b_copy, "wait_send")
        loop_copies(d_copy, "wait_send")

    forward(0)
    forward(1)
    w_start()
    backward(0)
    rs_y_start(0)
    query_part(0)
    rs_y_middle(0)
    w_line()
    backward(1)
    rs_y_start(1)
    rs_z_start(0)
    query_part(1)
    w_near()
    rs_y_middle(1)
    rs_z_middle(0)
    w_plane()
    rs_z_start(1)
    rs_end(0)
    rs_z_middle(1)
    w_pair()
    rs_end(1)
    w_end()
    fin_got(0)
    fin_got(1)
    for c in sends:
        c.wait_send()


def shards(queries, keys, values, out_weight, out_grad):
    dma = pltpu.SemaphoreType.DMA
    vm = pltpu.VMEM
    dq, dk, dv, dw = pl.pallas_call(
        kernel,
        out_shape=(
            jax.ShapeDtypeStruct((ROWS, D), F32),
            jax.ShapeDtypeStruct((LAT, D), F32),
            jax.ShapeDtypeStruct((LAT, D), F32),
            jax.ShapeDtypeStruct((2, 16, 16, D), BF),
        ),
        in_specs=[pl.BlockSpec(memory_space=pl.ANY)] * 5,
        out_specs=[pl.BlockSpec(memory_space=pltpu.VMEM)] * 4,
        scratch_shapes=[
            vm((2, 4, 4, 2, 2, LAT, 128), BF),
            vm((256, 256), BF),
            vm((256, D), BF),
            vm((ROWS, D), F32),
            vm((256, D), BF),
            vm((256, 256), BF),
            vm((256, 256), BF),
            vm((2, 4, 256, 512), F32),
            vm((2, 1024, 512), BF),
            vm((1024, 512), BF),
            vm((256, 256), BF),
            vm((128, 512), BF),
            vm((128, 512), BF),
            vm((512, 128), BF),
            vm((512, 128), BF),
            vm((2, 4, 4, 2, 2, LAT, 128), BF),
            vm((2, 2, 3, 4, 2, LAT, 128), BF),
            vm((2, 2, 3, 2, LAT, 128), BF),
            vm((2, 4, 2, 2, LAT, 128), BF),
            vm((2, 2, 2, LAT, 128), F32),
            vm((2, 2, 128, 128), F32),
            vm((16, 16, D), BF),
            vm((16, 16, D), BF),
            vm((4, 16, 128), BF),
            vm((16, 16, 128), BF),
            vm((4, 16, 128), BF),
            dma((7,)), dma((6,)), dma((6,)),
            dma((4, 4, 2, 4)), dma((4, 4, 2)),
            dma((2, 2, 3)), dma((2, 2, 3)), dma((2, 2, 3)), dma((2, 2, 3)),
            dma((2, 2)), dma((2, 2)), dma((2,)), dma((2,)),
            dma((16,)), dma((16,)), dma((16,)), dma((16,)), dma((4,)), dma((4,)), dma((16,)), dma((16,)),
            dma, dma,
        ],
        compiler_params=pltpu.CompilerParams(
            collective_id=0, has_side_effects=True, vmem_limit_bytes=48 * 1024 * 1024
        ),
        name="attend_back",
    )(queries[0], keys[0], values[0], out_weight, out_grad[0])
    return (dq[None], dk[None], dv[None], dw.reshape(D, D).astype(F32))


def solution(mesh):
    part = P("shape", "query", None)
    return jax.shard_map(
        shards,
        mesh=mesh,
        in_specs=(part, part, part, P(), part),
        out_specs=(part, part, part, P()),
        check_vma=False,
    )
```

```python
import math

import jax
import jax.numpy as jnp
from jax import lax
from jax.experimental import pallas as pl
from jax.experimental.pallas import tpu as pltpu
from jax.sharding import PartitionSpec as P

MESH = pl.DeviceIdType.MESH
BF = jnp.bfloat16
F32 = jnp.float32

ROWS = 128
LAT = 32
D = 512
HALF = 256
SHAPES = 16
SCALE = 1.0 / math.sqrt(64)
LOG2E = 1.4426950408889634


def nt(a, b):
    return lax.dot_general(a, b, (((1,), (1,)), ((), ())), preferred_element_type=F32)


def tn(a, b):
    return lax.dot_general(a, b, (((0,), (0,)), ((), ())), preferred_element_type=F32)


def nn(a, b):
    return lax.dot_general(a, b, (((1,), (0,)), ((), ())), preferred_element_type=F32)


def kernel(
    q_hbm, k_hbm, v_hbm, w_hbm, g_hbm,
    dq_out, dk_out, dv_out, dw_out,
    kv, q2, gb, gst, w_v, dat, da, s_ref, pb_ref, ds_ref, at, qbd, dbd, qst, dst,
    dkv, ry, rz, red, fin, dqs, wpart, w_a, w_b_src, w_b, w_c,
    loc, sib_s, sib_r, agz_s, agz_r, agy_s, agy_r, ry_s, ry_r, rz_s, rz_r, fin_s, fin_r, dq_s, dq_r,
    a_s, a_r, b_s, b_r, c_s, c_r, d_s, d_r, e_s, e_r,
):
    shape_at = lax.axis_index("shape")
    query_at = lax.axis_index("query")
    core = lax.rem(query_at, 2)
    other = 1 - core
    y = lax.rem(lax.div(query_at, 2), 4)
    zh = lax.div(query_at, 8)
    x = lax.rem(shape_at, 4)
    zl = lax.div(shape_at, 4)
    y1, y2, y3 = [lax.rem(y + i, 4) for i in (1, 2, 3)]
    z1, z2, z3 = [lax.rem(zh + i, 4) for i in (1, 2, 3)]
    sib = (shape_at, query_at + 1 - 2 * core)
    to_z = {1: (shape_at, z1 * 8 + y * 2 + core), -1: (shape_at, z3 * 8 + y * 2 + core)}
    to_y = {1: (shape_at, zh * 8 + y1 * 2 + core), -1: (shape_at, zh * 8 + y3 * 2 + core)}
    line = zh * 4 + zl
    plane = x * 4 + y

    def y_peer(i):
        return (shape_at, zh * 8 + i * 2 + core)

    def plane_peer(i):
        return (zl * 4 + lax.div(i, 4), zh * 8 + lax.rem(i, 4) * 2 + core)

    def line_peer(i):
        return (lax.rem(i, 4) * 4 + x, lax.div(i, 4) * 8 + y * 2 + core)

    def after(i, k):
        return lax.rem(i + k, 4)

    barrier = pltpu.get_barrier_semaphore()

    def greet(dev):
        pl.semaphore_signal(barrier, inc=1, device_id=dev, device_id_type=MESH)

    greet(to_z[1])
    greet(to_z[-1])
    for k in (1, 2, 3):
        greet(line_peer(zh * 4 + after(zl, k)))

    @pl.loop(1, 16)
    def _(i):
        greet(plane_peer(lax.rem(plane + i, 16)))

    greet(sib)

    mine = pl.ds(pl.multiple_of(core * HALF, HALF), HALF)
    theirs = pl.ds(pl.multiple_of(other * HALF, HALF), HALF)
    my_rows = pl.ds(pl.multiple_of(core * ROWS, ROWS), ROWS)

    def block_cols(c, b):
        return pl.ds(pl.multiple_of(c * HALF + b * 128, 128), 128)

    local = [pltpu.make_async_copy(g_hbm, gst, loc.at[0])]
    for b in range(2):
        for t, ref in enumerate((k_hbm, v_hbm)):
            local.append(
                pltpu.make_async_copy(ref.at[:, block_cols(core, b)], kv.at[b, zh, y, core, t], loc.at[1])
            )
    local.append(pltpu.make_async_copy(w_hbm.at[mine, :], w_v, loc.at[2]))
    local.append(pltpu.make_async_copy(q_hbm.at[:, mine], q2.at[my_rows, :], loc.at[3]))
    for c in local:
        c.start()
    local[0].wait()
    gb[my_rows, :] = gst[...].astype(BF)

    sends = []

    def remote(src, dst, ss, rs, dev):
        return pltpu.make_async_remote_copy(
            src_ref=src, dst_ref=dst, send_sem=ss, recv_sem=rs, device_id=dev, device_id_type=MESH
        )

    def send(src, dst, ss, rs, dev, wait=True):
        c = remote(src, dst, ss, rs, dev)
        c.start()
        if wait:
            sends.append(c)

    def got(ref, sem):
        remote(ref, ref, sem, sem, sib).wait_recv()

    def sent(ref, sem):
        remote(ref, ref, sem, sem, sib).wait_send()

    pl.semaphore_wait(barrier, 21)

    for b in range(2):
        for t, ref in enumerate((k_hbm, v_hbm)):
            send(ref.at[:, block_cols(other, b)], kv.at[b, zh, y, core, t], sib_s.at[0], sib_r.at[0], sib, False)
    send(gb.at[my_rows, :], gb.at[my_rows, :], sib_s.at[1], sib_r.at[1], sib)
    send(q_hbm.at[:, theirs], q2.at[my_rows, :], sib_s.at[2], sib_r.at[2], sib)

    low = lax.broadcasted_iota(jnp.int32, (256, 128), 1) < 64
    zero = jnp.zeros((64, 256), BF)

    def prepare(b):
        cols = slice(b * 128, b * 128 + 128)
        q_t = q2[:, cols].T
        for ref, part in ((qbd, q_t), (dbd, dat[cols, :])):
            ref[b, 0:64, 0:256] = part[0:64]
            ref[b, 0:64, 256:512] = zero
            ref[b, 64:128, 0:256] = zero
            ref[b, 64:128, 256:512] = part[64:128]
        none = jnp.zeros((256, 128), BF)
        for ref, part in ((qst, q2[:, cols]), (dst, da[:, cols])):
            ref[b, 0:256] = jnp.where(low, part, none)
            ref[b, 256:512] = jnp.where(low, none, part)

    def sub(z, yy, c):
        return kv.at[:, z, yy, c]

    def ag_copy_z(z, c, way):
        return remote(sub(z, y, c), sub(z, y, c), agz_s, agz_r.at[z, c], to_z[way])

    def ag_send_y(z, c):
        for k in (1, 3, 2):
            send(sub(z, y, c), sub(z, y, c), agy_s, agy_r.at[z], y_peer(after(y, k)), False)

    def ag_got_z(z, c):
        got(sub(z, y, c), agz_r.at[z, c])

    pltpu.make_async_copy(kv.at[:, zh, y, core], kv.at[:, zh, y, core], loc.at[1]).wait()

    @pl.when(core == 0)
    def _():
        ag_copy_z(zh, 0, 1).start()

    @pl.when(core == 1)
    def _():
        ag_copy_z(zh, 1, -1).start()

    got(sub(zh, y, other), sib_r.at[0])

    @pl.when(core == 1)
    def _():
        ag_copy_z(zh, 0, 1).start()

    @pl.when(core == 0)
    def _():
        ag_copy_z(zh, 1, -1).start()

    ag_copy_z(zh, 1, 1).start()
    ag_copy_z(zh, 0, -1).start()
    ag_send_y(zh, 0)
    ag_send_y(zh, 1)

    for c in local[5:]:
        c.wait()
    got(gb.at[pl.ds(pl.multiple_of(other * ROWS, ROWS), ROWS), :], sib_r.at[1])
    got(q2.at[pl.ds(pl.multiple_of(other * ROWS, ROWS), ROWS), :], sib_r.at[2])
    dat[...] = nt(w_v[...], gb[...]).astype(BF)
    da[...] = nt(gb[...], w_v[...]).astype(BF)
    prepare(0)
    prepare(1)

    ag_got_z(z3, 0)
    ag_copy_z(z3, 0, 1).start()
    ag_got_z(z1, 1)
    ag_copy_z(z1, 1, -1).start()
    ag_send_y(z3, 0)
    ag_send_y(z1, 1)
    ag_got_z(z3, 1)
    ag_send_y(z3, 1)
    ag_got_z(z1, 0)
    ag_send_y(z1, 0)
    for c in range(2):
        ag_got_z(z2, c)
        ag_send_y(z2, c)

    def keys_of(b, z):
        return kv[b, z, :, :, 0].reshape(256, 128)

    def values_of(b, z):
        return kv[b, z, :, :, 1].reshape(256, 128)

    def all_of(b, t):
        return kv[b, :, :, :, t].reshape(1024, 128)

    tops = [None, None]

    def scores(z):
        got(kv.at[:, z, 0:3], agy_r.at[z])
        for b in range(2):
            s = nn(keys_of(b, z), qbd[b])
            s_ref[b, z] = s
            m = jnp.max(s, axis=0, keepdims=True)
            tops[b] = m if tops[b] is None else jnp.maximum(tops[b], m)

    def forward(b):
        top = tops[b]
        total = None
        for r in range(4):
            e = jnp.exp2((s_ref[b, r] - top) * (SCALE * LOG2E))
            s_ref[b, r] = e
            m = jnp.sum(e, axis=0, keepdims=True)
            total = m if total is None else total + m
        inv = 1.0 / total
        for r in range(4):
            p = s_ref[b, r] * inv
            s_ref[b, r] = p
            pb_ref[b, r * 256 : r * 256 + 256] = p.astype(BF)
        a = tn(all_of(b, 1), pb_ref[b])
        at[b * 128 : b * 128 + 64, :] = a[0:64, 0:256].astype(BF)
        at[b * 128 + 64 : b * 128 + 128, :] = a[64:128, 256:512].astype(BF)

    def delta_of(b):
        cols = slice(b * 128, b * 128 + 128)
        prod = dat[cols, :].astype(F32) * at[cols, :].astype(F32)
        return jnp.concatenate(
            [jnp.sum(prod[0:64], axis=0, keepdims=True), jnp.sum(prod[64:128], axis=0, keepdims=True)], axis=1
        )

    def backward(b, z, delta):
        rows = pl.ds(pl.multiple_of(z * 256, 256), 256)
        dp = nn(values_of(b, z), dbd[b])
        ds = (s_ref[b, z] * (dp - delta)).astype(BF)
        ds_ref[b, rows] = ds
        dkv[b, z, :, :, 0] = (nn(ds, qst[b]) * SCALE).astype(BF).reshape(4, 2, LAT, 128)
        dkv[b, z, :, :, 1] = nn(pb_ref[b, rows], dst[b]).astype(BF).reshape(4, 2, LAT, 128)

    def query_part(b):
        a = tn(all_of(b, 0), ds_ref[b]) * SCALE
        for c in range(2):
            rows = slice(c * 128, c * 128 + 128)
            dqs[b, c] = jnp.concatenate([a[0:64, rows], a[64:128, 256 + c * 128 : 384 + c * 128]], axis=0).T
        dq_out[:, block_cols(core, b)] = dqs[b, core]
        send(dqs.at[b, other], dq_out.at[:, block_cols(core, b)], dq_s, dq_r, sib, False)

    def add(*parts):
        out = parts[0].astype(F32)
        for p in parts[1:]:
            out = out + p.astype(F32)
        return out

    def rs_y(z):
        for k in (1, 3, 2):
            peer = after(y, k)
            send(dkv.at[:, z, peer], ry.at[z, y], ry_s, ry_r.at[z], y_peer(peer), False)

    def y_sum(z):
        got(ry.at[z, 0:3], ry_r.at[z])
        red[:, z] = add(dkv[:, z, y], ry[z, y1], ry[z, y3], ry[z, y2]).astype(BF)

    def z_send(z, c, i, k):
        send(red.at[:, z, c], rz.at[i, k], rz_s.at[i, k], rz_r.at[i, k], to_z[1 - 2 * i])

    def z_got(i, k):
        got(rz.at[i, k], rz_r.at[i, k])

    def rs_z_far():
        y_sum(z2)
        z_send(z2, 0, 0, 0)
        z_send(z2, 1, 1, 0)

    def rs_z_near():
        y_sum(z1)
        z_send(z1, 1, 0, 1)
        y_sum(z3)
        z_send(z3, 0, 1, 1)

    def rs_z_last():
        z_got(0, 0)
        red[:, z1, 0] = add(red[:, z1, 0], rz[0, 0]).astype(BF)
        z_send(z1, 0, 0, 2)
        z_got(1, 0)
        red[:, z3, 1] = add(red[:, z3, 1], rz[1, 0]).astype(BF)
        z_send(z3, 1, 1, 2)

    def rs_end():
        z_got(0, 1)
        z_got(1, 1)
        z_got(0, 2)
        fin[0] = add(red[:, zh, 0], rz[0, 2], rz[1, 1])
        z_got(1, 2)
        fin[1] = add(red[:, zh, 1], rz[0, 1], rz[1, 2])
        for t, out in enumerate((dk_out, dv_out)):
            for b in range(2):
                send(fin.at[other, b, t], out.at[:, block_cols(core, b)], fin_s, fin_r.at[t], sib, False)
                out[:, block_cols(core, b)] = fin[core, b, t]

    def rs_got():
        for t, out in enumerate((dk_out, dv_out)):
            got(out.at[:, theirs], fin_r.at[t])
        got(dq_out.at[:, theirs], dq_r)

    def spread(at_me, make):
        @pl.loop(1, 16)
        def _(i):
            make(lax.rem(at_me + i, 16)).start()

    def w_start():
        wpart[...] = nn(at[...], gb[...]).astype(BF).reshape(16, 16, D)
        spread(plane, lambda i: remote(wpart.at[i], w_a.at[plane], a_s, a_r, plane_peer(i)))
        w_a[plane] = wpart[plane]

    def w_to_line():
        got(w_a.at[0:15], a_r)
        total = jnp.sum(w_a[...].astype(F32), axis=0)
        for p in range(4):
            w_b_src[p] = total[:, p * 128 : p * 128 + 128].astype(BF)
        spread(line, lambda i: remote(w_b_src.at[lax.rem(i, 4)], w_b.at[line], b_s, b_r, line_peer(i)))
        w_b[line] = w_b_src[zl]

    def w_to_near():
        got(w_b.at[0:15], b_r)
        w_c[zl] = (jnp.sum(w_b[...].astype(F32), axis=0) * (1.0 / SHAPES)).astype(BF)
        for k in (1, 3, 2):
            send(w_c.at[zl], w_c.at[zl], c_s, c_r, line_peer(zh * 4 + after(zl, k)), False)

    def w_back():
        got(w_c.at[0:3], c_r)
        for p in range(4):
            dw_out[core, plane, :, p * 128 : p * 128 + 128] = w_c[p]
        spread(plane, lambda i: remote(dw_out.at[core, plane], dw_out.at[core, plane], d_s, d_r, plane_peer(i)))

    def w_pair():
        got(dw_out.at[core, 0:15], d_r)
        send(dw_out.at[core], dw_out.at[core], e_s, e_r, sib)

    def back(z):
        for b in range(2):
            backward(b, z, deltas[b])
        rs_y(z)

    for z in (zh, z3, z1, z2):
        scores(z)
    forward(0)
    forward(1)
    w_start()
    deltas = (delta_of(0), delta_of(1))
    for z in (z2, z1, z3, zh):
        back(z)
    query_part(0)
    query_part(1)
    w_to_line()
    rs_z_far()
    rs_z_near()
    y_sum(zh)
    w_to_near()
    rs_z_last()
    w_back()
    rs_end()
    w_pair()
    rs_got()
    got(dw_out.at[other], e_r)

    sent(sub(zh, y, other), sib_s.at[0])
    sent(kv.at[:, 0, 0:3], agz_s)
    sent(kv.at[:, 0:3], agy_s)
    sent(dkv.at[:, 0:3], ry_s)
    sent(fin.at[0], fin_s)
    sent(dqs.at[:, 0], dq_s)
    sent(w_a.at[0:15], a_s)
    sent(w_b.at[0:15], b_s)
    sent(w_c.at[0:3], c_s)
    sent(dw_out.at[core, 0:15], d_s)
    for c in sends:
        c.wait_send()


def finish(dq, dk, dv, dw, dq_out, dk_out, dv_out, dw_out):
    dq_out[...] = dq[...]
    dk_out[...] = dk[...]
    dv_out[...] = dv[...]
    dw_out[...] = dw[...].astype(F32)


def shards(queries, keys, values, out_weight, out_grad):
    dma = pltpu.SemaphoreType.DMA
    vm = pltpu.VMEM
    one = pl.BlockSpec(memory_space=pltpu.VMEM)
    sizes = ((ROWS, D), (LAT, D), (LAT, D))
    dq, dk, dv, dw = pl.pallas_call(
        kernel,
        out_shape=[jax.ShapeDtypeStruct(i, F32) for i in sizes] + [jax.ShapeDtypeStruct((2, 16, 16, D), BF)],
        in_specs=[pl.BlockSpec(memory_space=pltpu.HBM)] * 5,
        out_specs=[one] * 4,
        scratch_shapes=[
            vm((2, 4, 4, 2, 2, LAT, 128), BF),
            vm((256, 256), BF),
            vm((256, D), BF),
            vm((ROWS, D), F32),
            vm((256, D), BF),
            vm((256, 256), BF),
            vm((256, 256), BF),
            vm((2, 4, 256, 512), F32),
            vm((2, 1024, 512), BF),
            vm((2, 1024, 512), BF),
            vm((256, 256), BF),
            vm((2, 128, 512), BF),
            vm((2, 128, 512), BF),
            vm((2, 512, 128), BF),
            vm((2, 512, 128), BF),
            vm((2, 4, 4, 2, 2, LAT, 128), BF),
            vm((4, 4, 2, 2, 2, LAT, 128), BF),
            vm((2, 3, 2, 2, LAT, 128), BF),
            vm((2, 4, 2, 2, LAT, 128), BF),
            vm((2, 2, 2, LAT, 128), F32),
            vm((2, 2, 128, 128), F32),
            vm((16, 16, D), BF),
            vm((16, 16, D), BF),
            vm((4, 16, 128), BF),
            vm((16, 16, 128), BF),
            vm((4, 16, 128), BF),
            dma((4,)), dma((3,)), dma((3,)),
            dma, dma((4, 2)), dma, dma((4,)),
            dma, dma((4,)), dma((2, 3)), dma((2, 3)),
            dma, dma((2,)), dma, dma,
            dma, dma, dma, dma, dma, dma, dma, dma, dma, dma,
        ],
        compiler_params=pltpu.CompilerParams(
            collective_id=0, has_side_effects=True, vmem_limit_bytes=58 * 1024 * 1024
        ),
        name="attend_back",
    )(queries[0], keys[0], values[0], out_weight, out_grad[0])
    dq, dk, dv, dw = pl.pallas_call(
        finish,
        out_shape=[jax.ShapeDtypeStruct(i, F32) for i in sizes + ((D, D),)],
        in_specs=[one] * 4,
        out_specs=[one] * 4,
        compiler_params=pltpu.CompilerParams(vmem_limit_bytes=58 * 1024 * 1024),
        name="finish",
    )(dq, dk, dv, dw.reshape(D, D))
    return (dq[None], dk[None], dv[None], dw)


def solution(mesh):
    part = P("shape", "query", None)
    return jax.shard_map(
        shards,
        mesh=mesh,
        in_specs=(part, part, part, P(), part),
        out_specs=(part, part, part, P()),
        check_vma=False,
    )
```

```python
import math

import jax
import jax.numpy as jnp
from jax import lax
from jax.experimental import pallas as pl
from jax.experimental.pallas import tpu as pltpu
from jax.sharding import PartitionSpec as P

MESH = pl.DeviceIdType.MESH
BF = jnp.bfloat16
F32 = jnp.float32

ROWS = 128
LAT = 32
D = 512
HALF = 256
SHAPES = 16
SCALE = 1.0 / math.sqrt(64)
LOG2E = 1.4426950408889634
RING = (2, 1, 3)
PLANE = ((2, 2), (2, 1), (2, 3), (1, 2), (3, 2), (2, 0), (0, 2), (1, 1), (1, 3), (3, 1), (3, 3), (1, 0), (3, 0), (0, 1), (0, 3))
LINE = (8, 7, 9, 6, 10, 5, 11, 4, 12, 3, 13, 2, 14, 1, 15)


def nt(a, b):
    return lax.dot_general(a, b, (((1,), (1,)), ((), ())), preferred_element_type=F32)


def tn(a, b):
    return lax.dot_general(a, b, (((0,), (0,)), ((), ())), preferred_element_type=F32)


def nn(a, b):
    return lax.dot_general(a, b, (((1,), (0,)), ((), ())), preferred_element_type=F32)


def kernel(
    q_hbm, k_hbm, v_hbm, w_hbm, g_hbm,
    dq_out, dk_out, dv_out, dw_out,
    kv, q2, gb, gst, w_v, dat, da, s_ref, ap, ds_ref, at, qbd, dbd, qst, dst,
    dkv, ry, rz, red, fin, dqs, wpart, w_a, w_b_src, w_b, w_c, w_d,
    loc, sib_s, sib_r, agz_s, agz_r, agy_s, agy_r, ry_s, ry_r, rz_s, rz_r, fin_s, fin_r, dq_s, dq_r,
    a_s, a_r, b_s, b_r, c_s, c_r, d_s, d_r, e_s, e_r,
):
    shape_at = lax.axis_index("shape")
    query_at = lax.axis_index("query")
    core = lax.rem(query_at, 2)
    other = 1 - core
    y = lax.rem(lax.div(query_at, 2), 4)
    zh = lax.div(query_at, 8)
    x = lax.rem(shape_at, 4)
    zl = lax.div(shape_at, 4)
    y1, y2, y3 = [lax.rem(y + i, 4) for i in (1, 2, 3)]
    z1, z2, z3 = [lax.rem(zh + i, 4) for i in (1, 2, 3)]
    sib = (shape_at, query_at + 1 - 2 * core)
    to_z = {1: (shape_at, z1 * 8 + y * 2 + core), -1: (shape_at, z3 * 8 + y * 2 + core)}
    to_y = {1: (shape_at, zh * 8 + y1 * 2 + core), -1: (shape_at, zh * 8 + y3 * 2 + core)}
    def after(i, k):
        return lax.rem(i + k, 4)

    line = zh * 4 + zl
    plane = x * 4 + y

    def y_peer(i):
        return (shape_at, zh * 8 + i * 2 + core)

    def plane_at(d):
        return after(x, d[0]) * 4 + after(y, d[1])

    def plane_peer(d):
        return (zl * 4 + after(x, d[0]), zh * 8 + after(y, d[1]) * 2 + core)

    def line_peer(i):
        return (lax.rem(i, 4) * 4 + x, lax.div(i, 4) * 8 + y * 2 + core)

    barrier = pltpu.get_barrier_semaphore()

    def greet(dev):
        pl.semaphore_signal(barrier, inc=1, device_id=dev, device_id_type=MESH)

    greet(to_z[1])
    greet(to_z[-1])
    for k in (1, 2, 3):
        greet(line_peer(zh * 4 + after(zl, k)))

    for d in PLANE:
        greet(plane_peer(d))
    greet(sib)

    mine = pl.ds(pl.multiple_of(core * HALF, HALF), HALF)
    theirs = pl.ds(pl.multiple_of(other * HALF, HALF), HALF)
    my_rows = pl.ds(pl.multiple_of(core * ROWS, ROWS), ROWS)

    def block_cols(c, b):
        return pl.ds(pl.multiple_of(c * HALF + b * 128, 128), 128)

    local = [pltpu.make_async_copy(g_hbm, gst, loc.at[0])]
    for b in range(2):
        for t, ref in enumerate((k_hbm, v_hbm)):
            local.append(
                pltpu.make_async_copy(ref.at[:, block_cols(core, b)], kv.at[b, zh, y, core, t], loc.at[1])
            )
    local.append(pltpu.make_async_copy(w_hbm.at[mine, :], w_v, loc.at[2]))
    local.append(pltpu.make_async_copy(q_hbm.at[:, mine], q2.at[my_rows, :], loc.at[3]))
    for c in local:
        c.start()
    local[0].wait()
    gb[my_rows, :] = gst[...].astype(BF)

    sends = []
    kept = []

    def keep(src, dst):
        c = pltpu.make_async_copy(src, dst, loc.at[4 + len(kept)])
        c.start()
        kept.append(c)

    def remote(src, dst, ss, rs, dev):
        return pltpu.make_async_remote_copy(
            src_ref=src, dst_ref=dst, send_sem=ss, recv_sem=rs, device_id=dev, device_id_type=MESH
        )

    def send(src, dst, ss, rs, dev, wait=True):
        c = remote(src, dst, ss, rs, dev)
        c.start()
        if wait:
            sends.append(c)

    def got(ref, sem):
        remote(ref, ref, sem, sem, sib).wait_recv()

    def sent(ref, sem):
        remote(ref, ref, sem, sem, sib).wait_send()

    pl.semaphore_wait(barrier, 21)

    for b in range(2):
        for t, ref in enumerate((k_hbm, v_hbm)):
            send(ref.at[:, block_cols(other, b)], kv.at[b, zh, y, core, t], sib_s.at[0], sib_r.at[0], sib, False)
    send(gb.at[my_rows, :], gb.at[my_rows, :], sib_s.at[1], sib_r.at[1], sib)
    send(q_hbm.at[:, theirs], q2.at[my_rows, :], sib_s.at[2], sib_r.at[2], sib)

    low = lax.broadcasted_iota(jnp.int32, (256, 128), 1) < 64
    zero = jnp.zeros((64, 256), BF)

    def prepare(b):
        cols = slice(b * 128, b * 128 + 128)
        q_t = q2[:, cols].T
        for ref, part in ((qbd, q_t), (dbd, dat[cols, :])):
            ref[b, 0:64, 0:256] = part[0:64]
            ref[b, 0:64, 256:512] = zero
            ref[b, 64:128, 0:256] = zero
            ref[b, 64:128, 256:512] = part[64:128]
        none = jnp.zeros((256, 128), BF)
        for ref, part in ((qst, q2[:, cols]), (dst, da[:, cols])):
            ref[b, 0:256] = jnp.where(low, part, none)
            ref[b, 256:512] = jnp.where(low, none, part)

    def sub(z, yy, c):
        return kv.at[:, z, yy, c]

    def ag_z(ref, way, sem):
        return remote(ref, ref, agz_s, agz_r.at[sem], to_z[way])

    def ag_send_y(ref, sem):
        for k in RING:
            send(ref, ref, agy_s, agy_r.at[sem], y_peer(after(y, k)), False)

    def half(z, c, b):
        return kv.at[b, z, y, c]

    def ag_ahead(c):
        for b in range(2):
            ag_z(half(zh, c, b), 1 - 2 * c, 3 * c + b).start()

    pltpu.make_async_copy(kv.at[:, zh, y, core], kv.at[:, zh, y, core], loc.at[1]).wait()
    for c in range(2):
        pl.when(core == c)(lambda c=c: ag_ahead(c))
    got(sub(zh, y, other), sib_r.at[0])
    for c in range(2):
        pl.when(core != c)(lambda c=c: ag_ahead(c))
    ag_z(sub(zh, y, 1), 1, 2).start()
    ag_z(sub(zh, y, 0), -1, 5).start()
    ag_send_y(kv.at[:, zh, y], 0)

    for c in local[5:]:
        c.wait()
    got(gb.at[pl.ds(pl.multiple_of(other * ROWS, ROWS), ROWS), :], sib_r.at[1])
    got(q2.at[pl.ds(pl.multiple_of(other * ROWS, ROWS), ROWS), :], sib_r.at[2])
    dat[...] = nt(w_v[...], gb[...]).astype(BF)
    da[...] = nt(gb[...], w_v[...]).astype(BF)
    prepare(0)
    prepare(1)

    for b in range(2):
        for z, c, way in ((z3, 0, 1), (z1, 1, -1)):
            got(half(z, c, b), agz_r.at[3 * c + b])
            ag_z(half(z, c, b), way, 6 + 2 * c + b).start()
            ag_send_y(half(z, c, b), 1 + c)
    for z, c in ((z3, 1), (z1, 0)):
        got(sub(z, y, c), agz_r.at[2 + 3 * (1 - c)])
        ag_send_y(sub(z, y, c), 2 - c)
    for b in range(2):
        for c in range(2):
            got(half(z2, c, b), agz_r.at[6 + 2 * c + b])
        ag_send_y(kv.at[b, z2, y], 3 + b)

    def keys_of(b, z):
        return kv[b, z, :, :, 0].reshape(256, 128)

    def values_of(b, z):
        return kv[b, z, :, :, 1].reshape(256, 128)

    def all_of(b, t):
        return kv[b, :, :, :, t].reshape(1024, 128)

    order = (zh, z3, z1, z2)
    tops, totals, gains = ([[None] * 2 for _ in range(4)] for _ in range(3))

    def score(i, b):
        sc = nn(keys_of(b, order[i]), qbd[b])
        top = jnp.max(sc, axis=0, keepdims=True)
        e = jnp.exp2((sc - top) * (SCALE * LOG2E))
        s_ref[b, i] = e
        tops[i][b] = top
        totals[i][b] = jnp.sum(e, axis=0, keepdims=True)
        a = tn(values_of(b, order[i]), e.astype(BF))
        ap[b, i, 0:64, :] = a[0:64, 0:256]
        ap[b, i, 64:128, :] = a[64:128, 256:512]

    def combine(b):
        top = tops[0][b]
        for i in range(1, 4):
            top = jnp.maximum(top, tops[i][b])
        f = [jnp.exp2((tops[i][b] - top) * (SCALE * LOG2E)) for i in range(4)]
        total = f[0] * totals[0][b]
        for i in range(1, 4):
            total = total + f[i] * totals[i][b]
        inv = 1.0 / total
        for i in range(4):
            gains[i][b] = f[i] * inv
        for h in range(2):
            a = None
            for i in range(4):
                part = ap[b, i, h * 64 : h * 64 + 64, :] * gains[i][b][:, h * 256 : h * 256 + 256]
                a = part if a is None else a + part
            at[b * 128 + h * 64 : b * 128 + h * 64 + 64, :] = a.astype(BF)

    def delta_of(b):
        cols = slice(b * 128, b * 128 + 128)
        prod = dat[cols, :].astype(F32) * at[cols, :].astype(F32)
        return jnp.concatenate(
            [jnp.sum(prod[0:64], axis=0, keepdims=True), jnp.sum(prod[64:128], axis=0, keepdims=True)], axis=1
        )

    def backward(i, b, delta):
        z = order[i]
        rows = pl.ds(pl.multiple_of(z * 256, 256), 256)
        p = s_ref[b, i] * gains[i][b]
        dp = nn(values_of(b, z), dbd[b])
        ds = (p * (dp - delta)).astype(BF)
        ds_ref[b, rows] = ds
        dkv[b, z, :, :, 0] = (nn(ds, qst[b]) * SCALE).astype(BF).reshape(4, 2, LAT, 128)
        dkv[b, z, :, :, 1] = nn(p.astype(BF), dst[b]).astype(BF).reshape(4, 2, LAT, 128)

    def query_part(b):
        a = tn(all_of(b, 0), ds_ref[b]) * SCALE
        for c in range(2):
            rows = slice(c * 128, c * 128 + 128)
            dqs[b, c] = jnp.concatenate([a[0:64, rows], a[64:128, 256 + c * 128 : 384 + c * 128]], axis=0).T
        keep(dqs.at[b, core], dq_out.at[:, block_cols(core, b)])
        send(dqs.at[b, other], dq_out.at[:, block_cols(core, b)], dq_s, dq_r, sib, False)

    def add(*parts):
        out = parts[0].astype(F32)
        for p in parts[1:]:
            out = out + p.astype(F32)
        return out

    def rs_y(z):
        for k in RING:
            peer = after(y, k)
            send(dkv.at[:, z, peer], ry.at[z, y], ry_s, ry_r.at[z], y_peer(peer), False)

    def y_sum(z):
        got(ry.at[z, 0:3], ry_r.at[z])
        red[:, z] = add(dkv[:, z, y], ry[z, y1], ry[z, y3], ry[z, y2]).astype(BF)

    def z_send(z, c, i, k):
        send(red.at[:, z, c], rz.at[i, k], rz_s.at[i, k], rz_r.at[i, k], to_z[1 - 2 * i])

    def z_got(i, k):
        got(rz.at[i, k], rz_r.at[i, k])

    def rs_z_far():
        y_sum(z2)
        z_send(z2, 0, 0, 0)
        z_send(z2, 1, 1, 0)

    def rs_z_near():
        y_sum(z1)
        z_send(z1, 1, 0, 1)
        y_sum(z3)
        z_send(z3, 0, 1, 1)

    def rs_z_last():
        z_got(0, 0)
        red[:, z1, 0] = add(red[:, z1, 0], rz[0, 0]).astype(BF)
        z_send(z1, 0, 0, 2)
        z_got(1, 0)
        red[:, z3, 1] = add(red[:, z3, 1], rz[1, 0]).astype(BF)
        z_send(z3, 1, 1, 2)

    def rs_end():
        z_got(0, 1)
        z_got(1, 1)
        z_got(0, 2)
        fin[0] = add(red[:, zh, 0], rz[0, 2], rz[1, 1])
        z_got(1, 2)
        fin[1] = add(red[:, zh, 1], rz[0, 1], rz[1, 2])
        for t, out in enumerate((dk_out, dv_out)):
            for b in range(2):
                send(fin.at[other, b, t], out.at[:, block_cols(core, b)], fin_s, fin_r.at[t], sib, False)
                keep(fin.at[core, b, t], out.at[:, block_cols(core, b)])

    def rs_got():
        for t, out in enumerate((dk_out, dv_out)):
            got(out.at[:, theirs], fin_r.at[t])
        got(dq_out.at[:, theirs], dq_r)

    def w_start():
        wpart[...] = nn(at[...], gb[...]).astype(BF).reshape(16, 16, D)
        for d in PLANE:
            send(wpart.at[plane_at(d)], w_a.at[plane], a_s, a_r, plane_peer(d), False)
        w_a[plane] = wpart[plane]

    def w_to_line():
        got(w_a.at[0:15], a_r)
        total = jnp.sum(w_a[...].astype(F32), axis=0)
        for p in range(4):
            w_b_src[p] = total[:, p * 128 : p * 128 + 128].astype(BF)
        for k in LINE:
            peer = lax.rem(line + k, 16)
            send(w_b_src.at[lax.rem(peer, 4)], w_b.at[line], b_s, b_r, line_peer(peer), False)
        w_b[line] = w_b_src[zl]

    def w_to_near():
        got(w_b.at[0:15], b_r)
        w_c[zl] = (jnp.sum(w_b[...].astype(F32), axis=0) * (1.0 / SHAPES)).astype(BF)
        for k in (1, 3, 2):
            send(w_c.at[zl], w_c.at[zl], c_s, c_r, line_peer(zh * 4 + after(zl, k)), False)

    def w_back():
        got(w_c.at[0:3], c_r)
        for p in range(4):
            w_d[plane, :, p * 128 : p * 128 + 128] = w_c[p]
        for d in PLANE:
            send(w_d.at[plane], w_d.at[plane], d_s, d_r, plane_peer(d), False)

    def w_pair():
        got(w_d.at[0:15], d_r)
        send(w_d, dw_out.at[core], e_s, e_r, sib)
        keep(w_d, dw_out.at[core])

    def back(i):
        for b in range(2):
            backward(i, b, deltas[b])
        rs_y(order[i])

    for i in range(3):
        got(kv.at[:, order[i], 0:3], agy_r.at[i])
        score(i, 0)
        score(i, 1)
    for b in range(2):
        got(kv.at[b, z2, 0:3], agy_r.at[3 + b])
        score(3, b)
        combine(b)
    w_start()
    deltas = (delta_of(0), delta_of(1))
    for i in (3, 2, 1, 0):
        back(i)
    query_part(0)
    query_part(1)
    w_to_line()
    rs_z_far()
    rs_z_near()
    y_sum(zh)
    w_to_near()
    rs_z_last()
    w_back()
    rs_end()
    w_pair()
    rs_got()
    got(dw_out.at[other], e_r)

    sent(sub(zh, y, other), sib_s.at[0])
    sent(kv.at[:, 0, 0:3], agz_s)
    sent(kv.at[:, 0:3], agy_s)
    sent(dkv.at[:, 0:3], ry_s)
    sent(fin.at[0], fin_s)
    sent(dqs.at[:, 0], dq_s)
    sent(w_a.at[0:15], a_s)
    sent(w_b.at[0:15], b_s)
    sent(w_c.at[0:3], c_s)
    sent(w_d.at[0:15], d_s)
    for c in kept:
        c.wait()
    for c in sends:
        c.wait_send()


def finish(dq, dk, dv, dw, dq_out, dk_out, dv_out, dw_out, vq, vk, vv, half, full, sem):
    rest = ((dq, vq, dq_out), (dk, vk, dk_out), (dv, vv, dv_out))
    loads = [pltpu.make_async_copy(dw.at[pl.ds(i * 128, 128)], half.at[i], sem.at[i]) for i in range(4)]
    loads += [pltpu.make_async_copy(src, mid, sem.at[4 + i]) for i, (src, mid, _) in enumerate(rest)]
    stores = [pltpu.make_async_copy(full.at[i], dw_out.at[pl.ds(i * 128, 128)], sem.at[7 + i]) for i in range(4)]
    stores += [pltpu.make_async_copy(mid, dst, sem.at[11 + i]) for i, (_, mid, dst) in enumerate(rest)]
    for c in loads:
        c.start()
    for i in range(7):
        loads[i].wait()
        if i < 4:
            full[i] = half[i].astype(F32)
        stores[i].start()
    for c in stores:
        c.wait()


def shards(queries, keys, values, out_weight, out_grad):
    dma = pltpu.SemaphoreType.DMA
    vm = pltpu.VMEM
    one = pl.BlockSpec(memory_space=pltpu.HBM)
    sizes = ((ROWS, D), (LAT, D), (LAT, D))
    dq, dk, dv, dw = pl.pallas_call(
        kernel,
        out_shape=[jax.ShapeDtypeStruct(i, F32) for i in sizes] + [jax.ShapeDtypeStruct((2, 16, 16, D), BF)],
        in_specs=[one] * 5,
        out_specs=[one] * 4,
        scratch_shapes=[
            vm((2, 4, 4, 2, 2, LAT, 128), BF),
            vm((256, 256), BF),
            vm((256, D), BF),
            vm((ROWS, D), F32),
            vm((256, D), BF),
            vm((256, 256), BF),
            vm((256, 256), BF),
            vm((2, 4, 256, 512), F32),
            vm((2, 4, 128, 256), F32),
            vm((2, 1024, 512), BF),
            vm((256, 256), BF),
            vm((2, 128, 512), BF),
            vm((2, 128, 512), BF),
            vm((2, 512, 128), BF),
            vm((2, 512, 128), BF),
            vm((2, 4, 4, 2, 2, LAT, 128), BF),
            vm((4, 4, 2, 2, 2, LAT, 128), BF),
            vm((2, 3, 2, 2, LAT, 128), BF),
            vm((2, 4, 2, 2, LAT, 128), BF),
            vm((2, 2, 2, LAT, 128), F32),
            vm((2, 2, 128, 128), F32),
            vm((16, 16, D), BF),
            vm((16, 16, D), BF),
            vm((4, 16, 128), BF),
            vm((16, 16, 128), BF),
            vm((4, 16, 128), BF),
            vm((16, 16, D), BF),
            dma((11,)), dma((3,)), dma((3,)),
            dma, dma((10,)), dma, dma((5,)),
            dma, dma((4,)), dma((2, 3)), dma((2, 3)),
            dma, dma((2,)), dma, dma,
            dma, dma, dma, dma, dma, dma, dma, dma, dma, dma,
        ],
        compiler_params=pltpu.CompilerParams(
            collective_id=0, has_side_effects=True, vmem_limit_bytes=58 * 1024 * 1024
        ),
        name="attend_back",
    )(queries[0], keys[0], values[0], out_weight, out_grad[0])
    dq, dk, dv, dw = pl.pallas_call(
        finish,
        out_shape=[jax.ShapeDtypeStruct(i, F32) for i in sizes + ((D, D),)],
        in_specs=[one] * 4,
        out_specs=[one] * 4,
        scratch_shapes=[vm(i, F32) for i in sizes] + [vm((4, 128, D), BF), vm((4, 128, D), F32), dma((14,))],
        compiler_params=pltpu.CompilerParams(vmem_limit_bytes=58 * 1024 * 1024),
        name="finish",
    )(dq, dk, dv, dw.reshape(D, D))
    return (dq[None], dk[None], dv[None], dw)


def solution(mesh):
    part = P("shape", "query", None)
    return jax.shard_map(
        shards,
        mesh=mesh,
        in_specs=(part, part, part, P(), part),
        out_specs=(part, part, part, P()),
        check_vma=False,
    )
```

```python
import math

import jax
import jax.numpy as jnp
from jax import lax
from jax.experimental import pallas as pl
from jax.experimental.pallas import tpu as pltpu
from jax.sharding import PartitionSpec as P

MESH = pl.DeviceIdType.MESH
BF = jnp.bfloat16
F32 = jnp.float32

ROWS = 128
LAT = 32
D = 512
HALF = 256
SHAPES = 16
SCALE = 1.0 / math.sqrt(64)
LOG2E = 1.4426950408889634
RING = (2, 1, 3)
PLANE = ((2, 2), (2, 1), (2, 3), (1, 2), (3, 2), (2, 0), (0, 2), (1, 1), (1, 3), (3, 1), (3, 3), (1, 0), (3, 0), (0, 1), (0, 3))
LINE = (8, 7, 9, 6, 10, 5, 11, 4, 12, 3, 13, 2, 14, 1, 15)


def nt(a, b):
    return lax.dot_general(a, b, (((1,), (1,)), ((), ())), preferred_element_type=F32)


def tn(a, b):
    return lax.dot_general(a, b, (((0,), (0,)), ((), ())), preferred_element_type=F32)


def nn(a, b):
    return lax.dot_general(a, b, (((1,), (0,)), ((), ())), preferred_element_type=F32)


def kernel(
    q_hbm, k_hbm, v_hbm, w_hbm, g_hbm,
    dq_out, dk_out, dv_out, dw_out,
    kv, q2, gb, gst, w_v, dat, da, s_ref, ap, ds_ref, at, qbd, dbd, qst, dst,
    dkv, ry, rz, red, fin, dqs, wpart, w_a, w_b_src, w_b, w_c, w_d,
    loc, sib_s, sib_r, agz_s, agz_r, agy_s, agy_r, ry_s, ry_r, rz_s, rz_r, fin_s, fin_r, dq_s, dq_r,
    a_s, a_r, b_s, b_r, c_s, c_r, d_s, d_r, e_s, e_r,
):
    shape_at = lax.axis_index("shape")
    query_at = lax.axis_index("query")
    core = lax.rem(query_at, 2)
    other = 1 - core
    y = lax.rem(lax.div(query_at, 2), 4)
    zh = lax.div(query_at, 8)
    x = lax.rem(shape_at, 4)
    zl = lax.div(shape_at, 4)
    y1, y2, y3 = [lax.rem(y + i, 4) for i in (1, 2, 3)]
    z1, z2, z3 = [lax.rem(zh + i, 4) for i in (1, 2, 3)]
    sib = (shape_at, query_at + 1 - 2 * core)
    to_z = {1: (shape_at, z1 * 8 + y * 2 + core), -1: (shape_at, z3 * 8 + y * 2 + core)}
    to_y = {1: (shape_at, zh * 8 + y1 * 2 + core), -1: (shape_at, zh * 8 + y3 * 2 + core)}
    def after(i, k):
        return lax.rem(i + k, 4)

    line = zh * 4 + zl
    plane = x * 4 + y

    def y_peer(i):
        return (shape_at, zh * 8 + i * 2 + core)

    def plane_at(d):
        return after(x, d[0]) * 4 + after(y, d[1])

    def plane_peer(d):
        return (zl * 4 + after(x, d[0]), zh * 8 + after(y, d[1]) * 2 + core)

    def line_peer(i):
        return (lax.rem(i, 4) * 4 + x, lax.div(i, 4) * 8 + y * 2 + core)

    barrier = pltpu.get_barrier_semaphore()

    def greet(dev):
        pl.semaphore_signal(barrier, inc=1, device_id=dev, device_id_type=MESH)

    greet(to_z[1])
    greet(to_z[-1])
    for k in (1, 2, 3):
        greet(line_peer(zh * 4 + after(zl, k)))

    for d in PLANE:
        greet(plane_peer(d))
    greet(sib)

    mine = pl.ds(pl.multiple_of(core * HALF, HALF), HALF)
    theirs = pl.ds(pl.multiple_of(other * HALF, HALF), HALF)
    my_rows = pl.ds(pl.multiple_of(core * ROWS, ROWS), ROWS)

    def block_cols(c, b):
        return pl.ds(pl.multiple_of(c * HALF + b * 128, 128), 128)

    local = [pltpu.make_async_copy(g_hbm, gst, loc.at[0])]
    for b in range(2):
        for t, ref in enumerate((k_hbm, v_hbm)):
            local.append(
                pltpu.make_async_copy(ref.at[:, block_cols(core, b)], kv.at[b, zh, y, core, t], loc.at[1])
            )
    local.append(pltpu.make_async_copy(w_hbm.at[mine, :], w_v, loc.at[2]))
    local.append(pltpu.make_async_copy(q_hbm.at[:, mine], q2.at[my_rows, :], loc.at[3]))
    for c in local:
        c.start()
    local[0].wait()
    gb[my_rows, :] = gst[...].astype(BF)

    sends = []
    kept = []

    def keep(src, dst):
        c = pltpu.make_async_copy(src, dst, loc.at[4 + len(kept)])
        c.start()
        kept.append(c)

    def remote(src, dst, ss, rs, dev):
        return pltpu.make_async_remote_copy(
            src_ref=src, dst_ref=dst, send_sem=ss, recv_sem=rs, device_id=dev, device_id_type=MESH
        )

    def send(src, dst, ss, rs, dev, wait=True):
        c = remote(src, dst, ss, rs, dev)
        c.start()
        if wait:
            sends.append(c)

    def got(ref, sem):
        remote(ref, ref, sem, sem, sib).wait_recv()

    def sent(ref, sem):
        remote(ref, ref, sem, sem, sib).wait_send()

    pl.semaphore_wait(barrier, 21)

    for b in range(2):
        for t, ref in enumerate((k_hbm, v_hbm)):
            send(ref.at[:, block_cols(other, b)], kv.at[b, zh, y, core, t], sib_s.at[0], sib_r.at[0], sib, False)
    send(gb.at[my_rows, :], gb.at[my_rows, :], sib_s.at[1], sib_r.at[1], sib)
    send(q_hbm.at[:, theirs], q2.at[my_rows, :], sib_s.at[2], sib_r.at[2], sib)

    low = lax.broadcasted_iota(jnp.int32, (256, 128), 1) < 64
    zero = jnp.zeros((64, 256), BF)

    def prepare(b):
        cols = slice(b * 128, b * 128 + 128)
        q_t = q2[:, cols].T
        for ref, part in ((qbd, q_t), (dbd, dat[cols, :])):
            ref[b, 0:64, 0:256] = part[0:64]
            ref[b, 0:64, 256:512] = zero
            ref[b, 64:128, 0:256] = zero
            ref[b, 64:128, 256:512] = part[64:128]
        none = jnp.zeros((256, 128), BF)
        for ref, part in ((qst, q2[:, cols]), (dst, da[:, cols])):
            ref[b, 0:256] = jnp.where(low, part, none)
            ref[b, 256:512] = jnp.where(low, none, part)

    def sub(z, yy, c):
        return kv.at[:, z, yy, c]

    def ag_z(ref, way, sem):
        return remote(ref, ref, agz_s, agz_r.at[sem], to_z[way])

    def ag_send_y(ref, sem):
        for k in RING:
            send(ref, ref, agy_s, agy_r.at[sem], y_peer(after(y, k)), False)

    def half(z, c, b):
        return kv.at[b, z, y, c]

    def ag_ahead(c):
        for b in range(2):
            ag_z(half(zh, c, b), 1 - 2 * c, 3 * c + b).start()

    pltpu.make_async_copy(kv.at[:, zh, y, core], kv.at[:, zh, y, core], loc.at[1]).wait()
    for c in range(2):
        pl.when(core == c)(lambda c=c: ag_ahead(c))
    got(sub(zh, y, other), sib_r.at[0])
    for c in range(2):
        pl.when(core != c)(lambda c=c: ag_ahead(c))
    ag_z(sub(zh, y, 1), 1, 2).start()
    ag_z(sub(zh, y, 0), -1, 5).start()
    ag_send_y(kv.at[:, zh, y], 0)

    for c in local[5:]:
        c.wait()
    got(gb.at[pl.ds(pl.multiple_of(other * ROWS, ROWS), ROWS), :], sib_r.at[1])
    got(q2.at[pl.ds(pl.multiple_of(other * ROWS, ROWS), ROWS), :], sib_r.at[2])
    dat[...] = nt(w_v[...], gb[...]).astype(BF)
    da[...] = nt(gb[...], w_v[...]).astype(BF)
    prepare(0)
    prepare(1)

    for b in range(2):
        for z, c, way in ((z3, 0, 1), (z1, 1, -1)):
            got(half(z, c, b), agz_r.at[3 * c + b])
            ag_z(half(z, c, b), way, 6 + 2 * c + b).start()
            ag_send_y(half(z, c, b), 1 + c)
    for z, c in ((z3, 1), (z1, 0)):
        got(sub(z, y, c), agz_r.at[2 + 3 * (1 - c)])
        ag_send_y(sub(z, y, c), 2 - c)
    for b in range(2):
        for c in range(2):
            got(half(z2, c, b), agz_r.at[6 + 2 * c + b])
        ag_send_y(kv.at[b, z2, y], 3 + b)

    def keys_of(b, z):
        return kv[b, z, :, :, 0].reshape(256, 128)

    def values_of(b, z):
        return kv[b, z, :, :, 1].reshape(256, 128)

    def all_of(b, t):
        return kv[b, :, :, :, t].reshape(1024, 128)

    order = (zh, z3, z1, z2)
    tops, totals, gains = ([[None] * 2 for _ in range(4)] for _ in range(3))

    def score(i, b):
        sc = nn(keys_of(b, order[i]), qbd[b])
        top = jnp.max(sc, axis=0, keepdims=True)
        e = jnp.exp2((sc - top) * (SCALE * LOG2E))
        s_ref[b, i] = e
        tops[i][b] = top
        totals[i][b] = jnp.sum(e, axis=0, keepdims=True)
        a = tn(values_of(b, order[i]), e.astype(BF))
        ap[b, i, 0:64, :] = a[0:64, 0:256]
        ap[b, i, 64:128, :] = a[64:128, 256:512]

    def combine(b):
        top = tops[0][b]
        for i in range(1, 4):
            top = jnp.maximum(top, tops[i][b])
        f = [jnp.exp2((tops[i][b] - top) * (SCALE * LOG2E)) for i in range(4)]
        total = f[0] * totals[0][b]
        for i in range(1, 4):
            total = total + f[i] * totals[i][b]
        inv = 1.0 / total
        for i in range(4):
            gains[i][b] = f[i] * inv
        for h in range(2):
            a = None
            for i in range(4):
                part = ap[b, i, h * 64 : h * 64 + 64, :] * gains[i][b][:, h * 256 : h * 256 + 256]
                a = part if a is None else a + part
            at[b * 128 + h * 64 : b * 128 + h * 64 + 64, :] = a.astype(BF)

    def delta_of(b):
        cols = slice(b * 128, b * 128 + 128)
        prod = dat[cols, :].astype(F32) * at[cols, :].astype(F32)
        return jnp.concatenate(
            [jnp.sum(prod[0:64], axis=0, keepdims=True), jnp.sum(prod[64:128], axis=0, keepdims=True)], axis=1
        )

    def backward(i, b, delta):
        z = order[i]
        rows = pl.ds(pl.multiple_of(z * 256, 256), 256)
        p = s_ref[b, i] * gains[i][b]
        dp = nn(values_of(b, z), dbd[b])
        ds = (p * (dp - delta)).astype(BF)
        ds_ref[b, rows] = ds
        dkv[b, z, :, :, 0] = (nn(ds, qst[b]) * SCALE).astype(BF).reshape(4, 2, LAT, 128)
        dkv[b, z, :, :, 1] = nn(p.astype(BF), dst[b]).astype(BF).reshape(4, 2, LAT, 128)

    def query_part(b):
        a = tn(all_of(b, 0), ds_ref[b]) * SCALE
        for c in range(2):
            rows = slice(c * 128, c * 128 + 128)
            dqs[b, c] = jnp.concatenate([a[0:64, rows], a[64:128, 256 + c * 128 : 384 + c * 128]], axis=0).T
        keep(dqs.at[b, core], dq_out.at[:, block_cols(core, b)])
        send(dqs.at[b, other], dq_out.at[:, block_cols(core, b)], dq_s, dq_r, sib, False)

    def add(*parts):
        out = parts[0].astype(F32)
        for p in parts[1:]:
            out = out + p.astype(F32)
        return out

    def rs_y(i):
        for k in RING:
            peer = after(y, k)
            send(dkv.at[:, order[i], peer], ry.at[i, y], ry_s, ry_r.at[i], y_peer(peer), False)

    def rs_y_far(b):
        for k in RING:
            peer = after(y, k)
            send(dkv.at[b, z2, peer], ry.at[3, y, b], ry_s, ry_r.at[3 + b], y_peer(peer), False)

    def y_sum(i):
        got(ry.at[i, 0:3], ry_r.at[i])
        red[:, order[i]] = add(dkv[:, order[i], y], ry[i, y1], ry[i, y3], ry[i, y2]).astype(BF)

    def z_send(src, dst, i, k):
        send(src, dst, rz_s.at[i, k], rz_r.at[i, k], to_z[1 - 2 * i])

    def rs_z_far(b):
        got(ry.at[3, 0:3, b], ry_r.at[3 + b])
        red[b, z2] = add(dkv[b, z2, y], ry[3, y1, b], ry[3, y3, b], ry[3, y2, b]).astype(BF)
        for c in range(2):
            z_send(red.at[b, z2, c], rz.at[c, 0, b], c, b)

    def rs_z_near():
        for i, z, c in ((2, z1, 0), (1, z3, 1)):
            y_sum(i)
            z_send(red.at[:, z, 1 - c], rz.at[c, 1], c, 2)

    def rs_z_last(b):
        for c, z in enumerate((z1, z3)):
            got(rz.at[c, 0, b], rz_r.at[c, b])
            red[b, z, c] = add(red[b, z, c], rz[c, 0, b]).astype(BF)
            z_send(red.at[b, z, c], rz.at[c, 2, b], c, 3 + b)

    def rs_end():
        for c in range(2):
            got(rz.at[c, 1], rz_r.at[c, 2])
            for b in range(2):
                got(rz.at[c, 2, b], rz_r.at[c, 3 + b])
        fin[0] = add(red[:, zh, 0], rz[0, 2], rz[1, 1])
        fin[1] = add(red[:, zh, 1], rz[0, 1], rz[1, 2])
        for t, out in enumerate((dk_out, dv_out)):
            for b in range(2):
                send(fin.at[other, b, t], out.at[:, block_cols(core, b)], fin_s, fin_r.at[t], sib, False)
                keep(fin.at[core, b, t], out.at[:, block_cols(core, b)])

    def rs_got():
        for t, out in enumerate((dk_out, dv_out)):
            got(out.at[:, theirs], fin_r.at[t])
        got(dq_out.at[:, theirs], dq_r)

    def w_start(b):
        rows = slice(b * 128, b * 128 + 128)
        wpart[b * 8 : b * 8 + 8] = nn(at[rows, :], gb[...]).astype(BF).reshape(8, 16, D)
        for k in (2, 1, 3, 0):
            for px in (2 * b, 2 * b + 1):
                peer = px * 4 + after(y, k)
                dev = (zl * 4 + px, zh * 8 + after(y, k) * 2 + core)
                c = remote(wpart.at[peer], w_a.at[plane], a_s, a_r, dev)
                if k == 0:
                    pl.when(px != x)(c.start)
                else:
                    c.start()

    def w_to_line():
        w_a[plane] = wpart[plane]
        got(w_a.at[0:15], a_r)
        total = jnp.sum(w_a[...].astype(F32), axis=0)
        for p in range(4):
            w_b_src[p] = total[:, p * 128 : p * 128 + 128].astype(BF)
        for k in LINE:
            peer = lax.rem(line + k, 16)
            send(w_b_src.at[lax.rem(peer, 4)], w_b.at[line], b_s, b_r, line_peer(peer), False)
        w_b[line] = w_b_src[zl]

    def w_to_near():
        got(w_b.at[0:15], b_r)
        w_c[zl] = (jnp.sum(w_b[...].astype(F32), axis=0) * (1.0 / SHAPES)).astype(BF)
        for k in (2, 1, 15):
            send(w_c.at[zl], w_c.at[zl], c_s, c_r, line_peer(lax.rem(line + k, 16)), False)

    def w_back():
        got(w_c.at[0:3], c_r)
        for p in range(4):
            w_d[plane, :, p * 128 : p * 128 + 128] = w_c[p]
        for d in PLANE:
            send(w_d.at[plane], w_d.at[plane], d_s, d_r, plane_peer(d), False)

    def w_pair():
        got(w_d.at[0:15], d_r)
        send(w_d, dw_out.at[core], e_s, e_r, sib)
        keep(w_d, dw_out.at[core])

    def back(i):
        for b in range(2):
            backward(i, b, deltas[b])
        rs_y(i)

    for i in range(3):
        got(kv.at[:, order[i], 0:3], agy_r.at[i])
        score(i, 0)
        score(i, 1)
    for b in range(2):
        got(kv.at[b, z2, 0:3], agy_r.at[3 + b])
        score(3, b)
        combine(b)
        w_start(b)
    deltas = (delta_of(0), delta_of(1))
    for b in range(2):
        backward(3, b, deltas[b])
        rs_y_far(b)
    for i in (2, 1, 0):
        back(i)
    query_part(0)
    query_part(1)
    w_to_line()
    rs_z_far(0)
    rs_z_far(1)
    w_to_near()
    rs_z_near()
    y_sum(0)
    rs_z_last(0)
    rs_z_last(1)
    w_back()
    w_pair()
    rs_end()
    rs_got()
    got(dw_out.at[other], e_r)

    sent(sub(zh, y, other), sib_s.at[0])
    sent(kv.at[:, 0, 0:3], agz_s)
    sent(kv.at[:, 0:3], agy_s)
    sent(dkv.at[:, 0:3], ry_s)
    sent(fin.at[0], fin_s)
    sent(dqs.at[:, 0], dq_s)
    sent(w_a.at[0:15], a_s)
    sent(w_b.at[0:15], b_s)
    sent(w_c.at[0:3], c_s)
    sent(w_d.at[0:15], d_s)
    for c in kept:
        c.wait()
    for c in sends:
        c.wait_send()


def finish(dq, dk, dv, dw, dq_out, dk_out, dv_out, dw_out, vq, vk, vv, half, full, sem):
    rest = ((dq, vq, dq_out), (dk, vk, dk_out), (dv, vv, dv_out))
    loads = [pltpu.make_async_copy(dw.at[pl.ds(i * 128, 128)], half.at[i], sem.at[i]) for i in range(4)]
    loads += [pltpu.make_async_copy(src, mid, sem.at[4 + i]) for i, (src, mid, _) in enumerate(rest)]
    stores = [pltpu.make_async_copy(full.at[i], dw_out.at[pl.ds(i * 128, 128)], sem.at[7 + i]) for i in range(4)]
    stores += [pltpu.make_async_copy(mid, dst, sem.at[11 + i]) for i, (_, mid, dst) in enumerate(rest)]
    for c in loads:
        c.start()
    for i in range(7):
        loads[i].wait()
        if i < 4:
            full[i] = half[i].astype(F32)
        stores[i].start()
    for c in stores:
        c.wait()


def shards(queries, keys, values, out_weight, out_grad):
    dma = pltpu.SemaphoreType.DMA
    vm = pltpu.VMEM
    one = pl.BlockSpec(memory_space=pltpu.HBM)
    sizes = ((ROWS, D), (LAT, D), (LAT, D))
    dq, dk, dv, dw = pl.pallas_call(
        kernel,
        out_shape=[jax.ShapeDtypeStruct(i, F32) for i in sizes] + [jax.ShapeDtypeStruct((2, 16, 16, D), BF)],
        in_specs=[one] * 5,
        out_specs=[one] * 4,
        scratch_shapes=[
            vm((2, 4, 4, 2, 2, LAT, 128), BF),
            vm((256, 256), BF),
            vm((256, D), BF),
            vm((ROWS, D), F32),
            vm((256, D), BF),
            vm((256, 256), BF),
            vm((256, 256), BF),
            vm((2, 4, 256, 512), F32),
            vm((2, 4, 128, 256), F32),
            vm((2, 1024, 512), BF),
            vm((256, 256), BF),
            vm((2, 128, 512), BF),
            vm((2, 128, 512), BF),
            vm((2, 512, 128), BF),
            vm((2, 512, 128), BF),
            vm((2, 4, 4, 2, 2, LAT, 128), BF),
            vm((4, 4, 2, 2, 2, LAT, 128), BF),
            vm((2, 3, 2, 2, LAT, 128), BF),
            vm((2, 4, 2, 2, LAT, 128), BF),
            vm((2, 2, 2, LAT, 128), F32),
            vm((2, 2, 128, 128), F32),
            vm((16, 16, D), BF),
            vm((16, 16, D), BF),
            vm((4, 16, 128), BF),
            vm((16, 16, 128), BF),
            vm((4, 16, 128), BF),
            vm((16, 16, D), BF),
            dma((11,)), dma((3,)), dma((3,)),
            dma, dma((10,)), dma, dma((5,)),
            dma, dma((5,)), dma((2, 5)), dma((2, 5)),
            dma, dma((2,)), dma, dma,
            dma, dma, dma, dma, dma, dma, dma, dma, dma, dma,
        ],
        compiler_params=pltpu.CompilerParams(
            collective_id=0, has_side_effects=True, vmem_limit_bytes=58 * 1024 * 1024
        ),
        name="attend_back",
    )(queries[0], keys[0], values[0], out_weight, out_grad[0])
    dq, dk, dv, dw = pl.pallas_call(
        finish,
        out_shape=[jax.ShapeDtypeStruct(i, F32) for i in sizes + ((D, D),)],
        in_specs=[one] * 4,
        out_specs=[one] * 4,
        scratch_shapes=[vm(i, F32) for i in sizes] + [vm((4, 128, D), BF), vm((4, 128, D), F32), dma((14,))],
        compiler_params=pltpu.CompilerParams(vmem_limit_bytes=58 * 1024 * 1024),
        name="finish",
    )(dq, dk, dv, dw.reshape(D, D))
    return (dq[None], dk[None], dv[None], dw)


def solution(mesh):
    part = P("shape", "query", None)
    return jax.shard_map(
        shards,
        mesh=mesh,
        in_specs=(part, part, part, P(), part),
        out_specs=(part, part, part, P()),
        check_vma=False,
    )
```

```python
import math

import jax
import jax.numpy as jnp
from jax import lax
from jax.experimental import pallas as pl
from jax.experimental.pallas import tpu as pltpu
from jax.sharding import PartitionSpec as P

MESH = pl.DeviceIdType.MESH
BF = jnp.bfloat16
F32 = jnp.float32

ROWS = 128
LAT = 32
D = 512
HALF = 256
SHAPES = 16
SCALE = 1.0 / math.sqrt(64)
LOG2E = 1.4426950408889634
RING = (2, 1, 3)
PLANE = ((2, 2), (2, 1), (2, 3), (1, 2), (3, 2), (2, 0), (0, 2), (1, 1), (1, 3), (3, 1), (3, 3), (1, 0), (3, 0), (0, 1), (0, 3))
LINE = (8, 7, 9, 6, 10, 5, 11, 4, 12, 3, 13, 2, 14, 1, 15)


def nt(a, b):
    return lax.dot_general(a, b, (((1,), (1,)), ((), ())), preferred_element_type=F32)


def tn(a, b):
    return lax.dot_general(a, b, (((0,), (0,)), ((), ())), preferred_element_type=F32)


def nn(a, b):
    return lax.dot_general(a, b, (((1,), (0,)), ((), ())), preferred_element_type=F32)


def kernel(
    q_hbm, k_hbm, v_hbm, w_hbm, g_hbm,
    dq_out, dk_out, dv_out, dw_out,
    kv, q2, gb, gst, w_v, dat, da, s_ref, ap, ds_ref, at, qbd, dbd, qst, dst,
    dkv, ry, rz, rzf, own, red, fin, dqs, wpart, w_a, w_b_src, w_b, w_c, w_d,
    loc, sib_s, sib_r, agz_s, agz_r, agy_s, agy_r, ry_s, ry_r, rz_s, rz_r, rf_r, fin_s, fin_r, dq_s, dq_r,
    a_s, a_r, b_s, b_r, c_s, c_r, d_s, d_r, e_s, e_r,
):
    shape_at = lax.axis_index("shape")
    query_at = lax.axis_index("query")
    core = lax.rem(query_at, 2)
    other = 1 - core
    y = lax.rem(lax.div(query_at, 2), 4)
    zh = lax.div(query_at, 8)
    x = lax.rem(shape_at, 4)
    zl = lax.div(shape_at, 4)
    y1, y2, y3 = [lax.rem(y + i, 4) for i in (1, 2, 3)]
    z1, z2, z3 = [lax.rem(zh + i, 4) for i in (1, 2, 3)]
    sib = (shape_at, query_at + 1 - 2 * core)
    to_z = {1: (shape_at, z1 * 8 + y * 2 + core), -1: (shape_at, z3 * 8 + y * 2 + core)}
    def to_z_core(way, c):
        return (shape_at, (z1 if way == 1 else z3) * 8 + y * 2 + c)

    to_y = {1: (shape_at, zh * 8 + y1 * 2 + core), -1: (shape_at, zh * 8 + y3 * 2 + core)}
    def after(i, k):
        return lax.rem(i + k, 4)

    line = zh * 4 + zl
    plane = x * 4 + y

    def y_peer(i):
        return (shape_at, zh * 8 + i * 2 + core)

    def plane_at(d):
        return after(x, d[0]) * 4 + after(y, d[1])

    def plane_peer(d):
        return (zl * 4 + after(x, d[0]), zh * 8 + after(y, d[1]) * 2 + core)

    def line_peer(i):
        return (lax.rem(i, 4) * 4 + x, lax.div(i, 4) * 8 + y * 2 + core)

    barrier = pltpu.get_barrier_semaphore()

    def greet(dev):
        pl.semaphore_signal(barrier, inc=1, device_id=dev, device_id_type=MESH)

    greet(to_z[1])
    greet(to_z[-1])
    for k in (1, 2, 3):
        greet(line_peer(zh * 4 + after(zl, k)))

    for d in PLANE:
        greet(plane_peer(d))
    greet(sib)

    mine = pl.ds(pl.multiple_of(core * HALF, HALF), HALF)
    theirs = pl.ds(pl.multiple_of(other * HALF, HALF), HALF)
    my_rows = pl.ds(pl.multiple_of(core * ROWS, ROWS), ROWS)

    def block_cols(c, b):
        return pl.ds(pl.multiple_of(c * HALF + b * 128, 128), 128)

    local = [pltpu.make_async_copy(g_hbm, gst, loc.at[0])]
    for b in range(2):
        for t, ref in enumerate((k_hbm, v_hbm)):
            local.append(
                pltpu.make_async_copy(ref.at[:, block_cols(core, b)], kv.at[b, zh, y, core, t], loc.at[1])
            )
    local.append(pltpu.make_async_copy(w_hbm.at[mine, :], w_v, loc.at[2]))
    local.append(pltpu.make_async_copy(q_hbm.at[:, mine], q2.at[my_rows, :], loc.at[3]))
    for c in local:
        c.start()
    local[0].wait()
    gb[my_rows, :] = gst[...].astype(BF)

    sends = []
    kept = []

    def keep(src, dst):
        c = pltpu.make_async_copy(src, dst, loc.at[4 + len(kept)])
        c.start()
        kept.append(c)

    def remote(src, dst, ss, rs, dev):
        return pltpu.make_async_remote_copy(
            src_ref=src, dst_ref=dst, send_sem=ss, recv_sem=rs, device_id=dev, device_id_type=MESH
        )

    def send(src, dst, ss, rs, dev, wait=True):
        c = remote(src, dst, ss, rs, dev)
        c.start()
        if wait:
            sends.append(c)

    def got(ref, sem):
        remote(ref, ref, sem, sem, sib).wait_recv()

    def sent(ref, sem):
        remote(ref, ref, sem, sem, sib).wait_send()

    pl.semaphore_wait(barrier, 21)

    for b in range(2):
        for t, ref in enumerate((k_hbm, v_hbm)):
            send(ref.at[:, block_cols(other, b)], kv.at[b, zh, y, core, t], sib_s.at[0], sib_r.at[0], sib, False)
    send(gb.at[my_rows, :], gb.at[my_rows, :], sib_s.at[1], sib_r.at[1], sib)
    send(q_hbm.at[:, theirs], q2.at[my_rows, :], sib_s.at[2], sib_r.at[2], sib)

    low = lax.broadcasted_iota(jnp.int32, (256, 128), 1) < 64
    zero = jnp.zeros((64, 256), BF)

    def prepare(b):
        cols = slice(b * 128, b * 128 + 128)
        q_t = q2[:, cols].T
        for ref, part in ((qbd, q_t), (dbd, dat[cols, :])):
            ref[b, 0:64, 0:256] = part[0:64]
            ref[b, 0:64, 256:512] = zero
            ref[b, 64:128, 0:256] = zero
            ref[b, 64:128, 256:512] = part[64:128]
        none = jnp.zeros((256, 128), BF)
        for ref, part in ((qst, q2[:, cols]), (dst, da[:, cols])):
            ref[b, 0:256] = jnp.where(low, part, none)
            ref[b, 256:512] = jnp.where(low, none, part)

    def sub(z, yy, c):
        return kv.at[:, z, yy, c]

    def ag_z(ref, way, sem):
        return remote(ref, ref, agz_s, agz_r.at[sem], to_z[way])

    def ag_send_y(ref, sem):
        for k in RING:
            send(ref, ref, agy_s, agy_r.at[sem], y_peer(after(y, k)), False)

    def half(z, c, b):
        return kv.at[b, z, y, c]

    def ag_ahead(c):
        for b in range(2):
            ag_z(half(zh, c, b), 1 - 2 * c, 3 * c + b).start()

    pltpu.make_async_copy(kv.at[:, zh, y, core], kv.at[:, zh, y, core], loc.at[1]).wait()
    for c in range(2):
        pl.when(core == c)(lambda c=c: ag_ahead(c))
    got(sub(zh, y, other), sib_r.at[0])
    for c in range(2):
        pl.when(core != c)(lambda c=c: ag_ahead(c))
    ag_z(sub(zh, y, 1), 1, 2).start()
    ag_z(sub(zh, y, 0), -1, 5).start()
    ag_send_y(kv.at[:, zh, y], 0)

    for c in local[5:]:
        c.wait()
    got(gb.at[pl.ds(pl.multiple_of(other * ROWS, ROWS), ROWS), :], sib_r.at[1])
    got(q2.at[pl.ds(pl.multiple_of(other * ROWS, ROWS), ROWS), :], sib_r.at[2])
    dat[...] = nt(w_v[...], gb[...]).astype(BF)
    da[...] = nt(gb[...], w_v[...]).astype(BF)
    prepare(0)
    prepare(1)

    for b in range(2):
        for z, c, way in ((z3, 0, 1), (z1, 1, -1)):
            got(half(z, c, b), agz_r.at[3 * c + b])
            ag_z(half(z, c, b), way, 6 + 2 * c + b).start()
            ag_send_y(half(z, c, b), 1 + c)
    for z, c in ((z3, 1), (z1, 0)):
        got(sub(z, y, c), agz_r.at[2 + 3 * (1 - c)])
        ag_send_y(sub(z, y, c), 2 - c)
    for b in range(2):
        for c in range(2):
            got(half(z2, c, b), agz_r.at[6 + 2 * c + b])
        ag_send_y(kv.at[b, z2, y], 3 + b)

    def keys_of(b, z):
        return kv[b, z, :, :, 0].reshape(256, 128)

    def values_of(b, z):
        return kv[b, z, :, :, 1].reshape(256, 128)

    def all_of(b, t):
        return kv[b, :, :, :, t].reshape(1024, 128)

    order = (zh, z3, z1, z2)
    tops, totals, gains = ([[None] * 2 for _ in range(4)] for _ in range(3))

    def score(i, b):
        sc = nn(keys_of(b, order[i]), qbd[b])
        top = jnp.max(sc, axis=0, keepdims=True)
        e = jnp.exp2((sc - top) * (SCALE * LOG2E))
        s_ref[b, i] = e
        tops[i][b] = top
        totals[i][b] = jnp.sum(e, axis=0, keepdims=True)
        a = tn(values_of(b, order[i]), e.astype(BF))
        ap[b, i, 0:64, :] = a[0:64, 0:256]
        ap[b, i, 64:128, :] = a[64:128, 256:512]

    def combine(b):
        top = tops[0][b]
        for i in range(1, 4):
            top = jnp.maximum(top, tops[i][b])
        f = [jnp.exp2((tops[i][b] - top) * (SCALE * LOG2E)) for i in range(4)]
        total = f[0] * totals[0][b]
        for i in range(1, 4):
            total = total + f[i] * totals[i][b]
        inv = 1.0 / total
        for i in range(4):
            gains[i][b] = f[i] * inv
        for h in range(2):
            a = None
            for i in range(4):
                part = ap[b, i, h * 64 : h * 64 + 64, :] * gains[i][b][:, h * 256 : h * 256 + 256]
                a = part if a is None else a + part
            at[b * 128 + h * 64 : b * 128 + h * 64 + 64, :] = a.astype(BF)

    def delta_of(b):
        cols = slice(b * 128, b * 128 + 128)
        prod = dat[cols, :].astype(F32) * at[cols, :].astype(F32)
        return jnp.concatenate(
            [jnp.sum(prod[0:64], axis=0, keepdims=True), jnp.sum(prod[64:128], axis=0, keepdims=True)], axis=1
        )

    def backward(i, b, delta):
        z = order[i]
        rows = pl.ds(pl.multiple_of(z * 256, 256), 256)
        p = s_ref[b, i] * gains[i][b]
        dp = nn(values_of(b, z), dbd[b])
        ds = (p * (dp - delta)).astype(BF)
        ds_ref[b, rows] = ds
        dkv[b, z, :, :, 0] = (nn(ds, qst[b]) * SCALE).astype(BF).reshape(4, 2, LAT, 128)
        dkv[b, z, :, :, 1] = nn(p.astype(BF), dst[b]).astype(BF).reshape(4, 2, LAT, 128)

    def query_part(b):
        a = tn(all_of(b, 0), ds_ref[b]) * SCALE
        for c in range(2):
            rows = slice(c * 128, c * 128 + 128)
            dqs[b, c] = jnp.concatenate([a[0:64, rows], a[64:128, 256 + c * 128 : 384 + c * 128]], axis=0).T
        keep(dqs.at[b, core], dq_out.at[:, block_cols(core, b)])
        send(dqs.at[b, other], dq_out.at[:, block_cols(core, b)], dq_s, dq_r, sib, False)

    def add(*parts):
        out = parts[0].astype(F32)
        for p in parts[1:]:
            out = out + p.astype(F32)
        return out

    def rs_y(i):
        for k in RING:
            peer = after(y, k)
            send(dkv.at[:, order[i], peer], ry.at[i, y], ry_s, ry_r.at[i], y_peer(peer), False)

    def rs_y_far(b):
        for k in RING:
            peer = after(y, k)
            send(dkv.at[b, z2, peer], ry.at[3, y, b], ry_s, ry_r.at[3 + b], y_peer(peer), False)

    def y_sum(i):
        got(ry.at[i, 0:3], ry_r.at[i])
        red[:, order[i]] = add(dkv[:, order[i], y], ry[i, y1], ry[i, y3], ry[i, y2]).astype(BF)

    def z_send(src, dst, i, k):
        send(src, dst, rz_s.at[i, k], rz_r.at[i, k], to_z[1 - 2 * i])

    def z_final(src, dst, c, i, k):
        send(src, dst, rz_s.at[i, k], rf_r.at[i], to_z_core(1 - 2 * i, c))

    def rs_z_far(b):
        got(ry.at[3, 0:3, b], ry_r.at[3 + b])
        red[b, z2] = add(dkv[b, z2, y], ry[3, y1, b], ry[3, y3, b], ry[3, y2, b]).astype(BF)
        for c in range(2):
            z_send(red.at[b, z2, c], rz.at[c, 0, b], c, b)

    def rs_z_near():
        for i, z, c in ((2, z1, 0), (1, z3, 1)):
            y_sum(i)
            z_final(red.at[:, z, 1 - c], rzf.at[c, core], 1 - c, c, 2)

    def rs_z_last(b):
        for c, z in enumerate((z1, z3)):
            got(rz.at[c, 0, b], rz_r.at[c, b])
            red[b, z, c] = add(red[b, z, c], rz[c, 0, b]).astype(BF)
            z_final(red.at[b, z, c], rzf.at[c, core, b], c, c, 3 + b)

    def rs_pair():
        y_sum(0)
        send(red.at[:, zh, other], own.at[core], fin_s, fin_r, sib, False)
        own[core] = red[:, zh, core]

    def rs_end():
        got(own.at[other], fin_r)
        for i in range(2):
            got(rzf.at[i], rf_r.at[i])
        for h in range(2):
            part = add(own[h], rzf[0, h], rzf[1, h])
            for b in range(2):
                cols = slice(h * HALF + b * 128, h * HALF + b * 128 + 128)
                fin[0, :, cols] = part[b, 0]
                fin[1, :, cols] = part[b, 1]
        keep(fin.at[0], dk_out)
        keep(fin.at[1], dv_out)

    def rs_got():
        got(dq_out.at[:, theirs], dq_r)

    def w_start(b):
        rows = slice(b * 128, b * 128 + 128)
        wpart[b * 8 : b * 8 + 8] = nn(at[rows, :], gb[...]).astype(BF).reshape(8, 16, D)
        for k in (2, 1, 3, 0):
            for px in (2 * b, 2 * b + 1):
                peer = px * 4 + after(y, k)
                dev = (zl * 4 + px, zh * 8 + after(y, k) * 2 + core)
                c = remote(wpart.at[peer], w_a.at[plane], a_s, a_r, dev)
                if k == 0:
                    pl.when(px != x)(c.start)
                else:
                    c.start()

    def w_to_line():
        w_a[plane] = wpart[plane]
        got(w_a.at[0:15], a_r)
        total = jnp.sum(w_a[...].astype(F32), axis=0)
        for p in range(4):
            w_b_src[p] = total[:, p * 128 : p * 128 + 128].astype(BF)
        for k in LINE:
            peer = lax.rem(line + k, 16)
            send(w_b_src.at[lax.rem(peer, 4)], w_b.at[line], b_s, b_r, line_peer(peer), False)
        w_b[line] = w_b_src[zl]

    def w_to_near():
        got(w_b.at[0:15], b_r)
        w_c[zl] = (jnp.sum(w_b[...].astype(F32), axis=0) * (1.0 / SHAPES)).astype(BF)
        for k in (2, 1, 15):
            send(w_c.at[zl], w_c.at[zl], c_s, c_r, line_peer(lax.rem(line + k, 16)), False)

    def w_back():
        got(w_c.at[0:3], c_r)
        for p in range(4):
            w_d[plane, :, p * 128 : p * 128 + 128] = w_c[p]
        for d in PLANE:
            send(w_d.at[plane], w_d.at[plane], d_s, d_r, plane_peer(d), False)

    def w_pair():
        got(w_d.at[0:15], d_r)
        send(w_d, dw_out.at[core], e_s, e_r, sib)
        keep(w_d, dw_out.at[core])

    def back(i):
        for b in range(2):
            backward(i, b, deltas[b])
        rs_y(i)

    for i in range(3):
        got(kv.at[:, order[i], 0:3], agy_r.at[i])
        score(i, 0)
        score(i, 1)
    for b in range(2):
        got(kv.at[b, z2, 0:3], agy_r.at[3 + b])
        score(3, b)
        combine(b)
        w_start(b)
    deltas = (delta_of(0), delta_of(1))
    for b in range(2):
        backward(3, b, deltas[b])
        rs_y_far(b)
    for i in (2, 1, 0):
        back(i)
    query_part(0)
    query_part(1)
    w_to_line()
    rs_z_far(0)
    rs_z_far(1)
    w_to_near()
    rs_z_near()
    rs_pair()
    rs_z_last(0)
    rs_z_last(1)
    w_back()
    w_pair()
    rs_end()
    rs_got()
    got(dw_out.at[other], e_r)

    sent(sub(zh, y, other), sib_s.at[0])
    sent(kv.at[:, 0, 0:3], agz_s)
    sent(kv.at[:, 0:3], agy_s)
    sent(dkv.at[:, 0:3], ry_s)
    sent(own.at[0], fin_s)
    sent(dqs.at[:, 0], dq_s)
    sent(w_a.at[0:15], a_s)
    sent(w_b.at[0:15], b_s)
    sent(w_c.at[0:3], c_s)
    sent(w_d.at[0:15], d_s)
    for c in kept:
        c.wait()
    for c in sends:
        c.wait_send()


def finish(dq, dk, dv, dw, dq_out, dk_out, dv_out, dw_out, vq, vk, vv, half, full, sem):
    rest = ((dq, vq, dq_out), (dk, vk, dk_out), (dv, vv, dv_out))
    loads = [pltpu.make_async_copy(dw.at[pl.ds(i * 128, 128)], half.at[i], sem.at[i]) for i in range(4)]
    loads += [pltpu.make_async_copy(src, mid, sem.at[4 + i]) for i, (src, mid, _) in enumerate(rest)]
    stores = [pltpu.make_async_copy(full.at[i], dw_out.at[pl.ds(i * 128, 128)], sem.at[7 + i]) for i in range(4)]
    stores += [pltpu.make_async_copy(mid, dst, sem.at[11 + i]) for i, (_, mid, dst) in enumerate(rest)]
    for c in loads:
        c.start()
    for i in range(7):
        loads[i].wait()
        if i < 4:
            full[i] = half[i].astype(F32)
        stores[i].start()
    for c in stores:
        c.wait()


def shards(queries, keys, values, out_weight, out_grad):
    dma = pltpu.SemaphoreType.DMA
    vm = pltpu.VMEM
    one = pl.BlockSpec(memory_space=pltpu.HBM)
    sizes = ((ROWS, D), (LAT, D), (LAT, D))
    dq, dk, dv, dw = pl.pallas_call(
        kernel,
        out_shape=[jax.ShapeDtypeStruct(i, F32) for i in sizes] + [jax.ShapeDtypeStruct((2, 16, 16, D), BF)],
        in_specs=[one] * 5,
        out_specs=[one] * 4,
        scratch_shapes=[
            vm((2, 4, 4, 2, 2, LAT, 128), BF),
            vm((256, 256), BF),
            vm((256, D), BF),
            vm((ROWS, D), F32),
            vm((256, D), BF),
            vm((256, 256), BF),
            vm((256, 256), BF),
            vm((2, 4, 256, 512), F32),
            vm((2, 4, 128, 256), F32),
            vm((2, 1024, 512), BF),
            vm((256, 256), BF),
            vm((2, 128, 512), BF),
            vm((2, 128, 512), BF),
            vm((2, 512, 128), BF),
            vm((2, 512, 128), BF),
            vm((2, 4, 4, 2, 2, LAT, 128), BF),
            vm((4, 4, 2, 2, 2, LAT, 128), BF),
            vm((2, 1, 2, 2, LAT, 128), BF),
            vm((2, 2, 2, 2, LAT, 128), BF),
            vm((2, 2, 2, LAT, 128), BF),
            vm((2, 4, 2, 2, LAT, 128), BF),
            vm((2, LAT, D), F32),
            vm((2, 2, 128, 128), F32),
            vm((16, 16, D), BF),
            vm((16, 16, D), BF),
            vm((4, 16, 128), BF),
            vm((16, 16, 128), BF),
            vm((4, 16, 128), BF),
            vm((16, 16, D), BF),
            dma((11,)), dma((3,)), dma((3,)),
            dma, dma((10,)), dma, dma((5,)),
            dma, dma((5,)), dma((2, 5)), dma((2, 2)), dma((2,)),
            dma, dma, dma, dma,
            dma, dma, dma, dma, dma, dma, dma, dma, dma, dma,
        ],
        compiler_params=pltpu.CompilerParams(
            collective_id=0, has_side_effects=True, vmem_limit_bytes=58 * 1024 * 1024
        ),
        name="attend_back",
    )(queries[0], keys[0], values[0], out_weight, out_grad[0])
    dq, dk, dv, dw = pl.pallas_call(
        finish,
        out_shape=[jax.ShapeDtypeStruct(i, F32) for i in sizes + ((D, D),)],
        in_specs=[one] * 4,
        out_specs=[one] * 4,
        scratch_shapes=[vm(i, F32) for i in sizes] + [vm((4, 128, D), BF), vm((4, 128, D), F32), dma((14,))],
        compiler_params=pltpu.CompilerParams(vmem_limit_bytes=58 * 1024 * 1024),
        name="finish",
    )(dq, dk, dv, dw.reshape(D, D))
    return (dq[None], dk[None], dv[None], dw)


def solution(mesh):
    part = P("shape", "query", None)
    return jax.shard_map(
        shards,
        mesh=mesh,
        in_specs=(part, part, part, P(), part),
        out_specs=(part, part, part, P()),
        check_vma=False,
    )
```

```python
import math

import jax
import jax.numpy as jnp
from jax import lax
from jax.experimental import pallas as pl
from jax.experimental.pallas import tpu as pltpu
from jax.sharding import PartitionSpec as P

MESH = pl.DeviceIdType.MESH
BF = jnp.bfloat16
F32 = jnp.float32

ROWS = 128
LAT = 32
D = 512
HALF = 256
SHAPES = 16
SCALE = 1.0 / math.sqrt(64)
LOG2E = 1.4426950408889634
RING = (2, 1, 3)
PLANE = ((2, 2), (2, 1), (2, 3), (1, 2), (3, 2), (2, 0), (0, 2), (1, 1), (1, 3), (3, 1), (3, 3), (1, 0), (3, 0), (0, 1), (0, 3))
LINE = (8, 7, 9, 6, 10, 5, 11, 4, 12, 3, 13, 2, 14, 1, 15)


def nt(a, b):
    return lax.dot_general(a, b, (((1,), (1,)), ((), ())), preferred_element_type=F32)


def tn(a, b):
    return lax.dot_general(a, b, (((0,), (0,)), ((), ())), preferred_element_type=F32)


def nn(a, b):
    return lax.dot_general(a, b, (((1,), (0,)), ((), ())), preferred_element_type=F32)


def kernel(
    q_hbm, k_hbm, v_hbm, w_hbm, g_hbm,
    dq_out, dk_out, dv_out, dw_out,
    kv, q2, gb, gst, w_v, dat, da, s_ref, ap, ds_ref, at, qbd, dbd, qst, dst,
    dkv, ry, rz, rzf, own, red, fin, dqs, wpart, w_a, w_b_src, w_b, w_c, w_d,
    loc, sib_s, sib_r, agz_s, agz_r, agy_s, agy_r, ry_s, ry_r, rz_s, rz_r, rf_r, fin_s, fin_r, dq_s, dq_r,
    a_s, a_r, b_s, b_r, c_s, c_r, d_s, d_r, e_s, e_r,
):
    shape_at = lax.axis_index("shape")
    query_at = lax.axis_index("query")
    core = lax.rem(query_at, 2)
    other = 1 - core
    y = lax.rem(lax.div(query_at, 2), 4)
    zh = lax.div(query_at, 8)
    x = lax.rem(shape_at, 4)
    zl = lax.div(shape_at, 4)
    y1, y2, y3 = [lax.rem(y + i, 4) for i in (1, 2, 3)]
    z1, z2, z3 = [lax.rem(zh + i, 4) for i in (1, 2, 3)]
    sib = (shape_at, query_at + 1 - 2 * core)
    to_z = {1: (shape_at, z1 * 8 + y * 2 + core), -1: (shape_at, z3 * 8 + y * 2 + core)}
    def to_z_core(way, c):
        return (shape_at, (z1 if way == 1 else z3) * 8 + y * 2 + c)

    to_y = {1: (shape_at, zh * 8 + y1 * 2 + core), -1: (shape_at, zh * 8 + y3 * 2 + core)}
    def after(i, k):
        return lax.rem(i + k, 4)

    line = zh * 4 + zl
    plane = x * 4 + y

    def y_peer(i):
        return (shape_at, zh * 8 + i * 2 + core)

    def plane_at(d):
        return after(x, d[0]) * 4 + after(y, d[1])

    def plane_peer(d):
        return (zl * 4 + after(x, d[0]), zh * 8 + after(y, d[1]) * 2 + core)

    def line_peer(i):
        return (lax.rem(i, 4) * 4 + x, lax.div(i, 4) * 8 + y * 2 + core)

    barrier = pltpu.get_barrier_semaphore()

    def greet(dev):
        pl.semaphore_signal(barrier, inc=1, device_id=dev, device_id_type=MESH)

    greet(to_z[1])
    greet(to_z[-1])
    for k in (1, 2, 3):
        greet(line_peer(zh * 4 + after(zl, k)))

    for d in PLANE:
        greet(plane_peer(d))
    greet(sib)

    mine = pl.ds(pl.multiple_of(core * HALF, HALF), HALF)
    theirs = pl.ds(pl.multiple_of(other * HALF, HALF), HALF)
    my_rows = pl.ds(pl.multiple_of(core * ROWS, ROWS), ROWS)

    def block_cols(c, b):
        return pl.ds(pl.multiple_of(c * HALF + b * 128, 128), 128)

    local = [pltpu.make_async_copy(g_hbm, gst, loc.at[0])]
    for b in range(2):
        for t, ref in enumerate((k_hbm, v_hbm)):
            local.append(
                pltpu.make_async_copy(ref.at[:, block_cols(core, b)], kv.at[b, zh, y, core, t], loc.at[1])
            )
    local.append(pltpu.make_async_copy(w_hbm.at[mine, :], w_v, loc.at[2]))
    local.append(pltpu.make_async_copy(q_hbm.at[:, mine], q2.at[my_rows, :], loc.at[3]))
    for c in local:
        c.start()
    local[0].wait()
    gb[my_rows, :] = gst[...].astype(BF)

    sends = []
    kept = []

    def keep(src, dst):
        c = pltpu.make_async_copy(src, dst, loc.at[4 + len(kept)])
        c.start()
        kept.append(c)

    def remote(src, dst, ss, rs, dev):
        return pltpu.make_async_remote_copy(
            src_ref=src, dst_ref=dst, send_sem=ss, recv_sem=rs, device_id=dev, device_id_type=MESH
        )

    def send(src, dst, ss, rs, dev, wait=True):
        c = remote(src, dst, ss, rs, dev)
        c.start()
        if wait:
            sends.append(c)

    def got(ref, sem):
        remote(ref, ref, sem, sem, sib).wait_recv()

    def sent(ref, sem):
        remote(ref, ref, sem, sem, sib).wait_send()

    pl.semaphore_wait(barrier, 21)

    for b in range(2):
        for t, ref in enumerate((k_hbm, v_hbm)):
            send(ref.at[:, block_cols(other, b)], kv.at[b, zh, y, core, t], sib_s.at[0], sib_r.at[0], sib, False)
    send(gb.at[my_rows, :], gb.at[my_rows, :], sib_s.at[1], sib_r.at[1], sib)
    send(q_hbm.at[:, theirs], q2.at[my_rows, :], sib_s.at[2], sib_r.at[2], sib)

    low = lax.broadcasted_iota(jnp.int32, (256, 128), 1) < 64
    zero = jnp.zeros((64, 256), BF)

    def prepare(b):
        cols = slice(b * 128, b * 128 + 128)
        q_t = q2[:, cols].T
        for ref, part in ((qbd, q_t), (dbd, dat[cols, :])):
            ref[b, 0:64, 0:256] = part[0:64]
            ref[b, 0:64, 256:512] = zero
            ref[b, 64:128, 0:256] = zero
            ref[b, 64:128, 256:512] = part[64:128]
        none = jnp.zeros((256, 128), BF)
        for ref, part in ((qst, q2[:, cols]), (dst, da[:, cols])):
            ref[b, 0:256] = jnp.where(low, part, none)
            ref[b, 256:512] = jnp.where(low, none, part)

    def sub(z, yy, c):
        return kv.at[:, z, yy, c]

    def ag_z(ref, way, sem):
        return remote(ref, ref, agz_s, agz_r.at[sem], to_z[way])

    def ag_send_y(ref, sem):
        for k in RING:
            send(ref, ref, agy_s, agy_r.at[sem], y_peer(after(y, k)), False)

    def half(z, c, b):
        return kv.at[b, z, y, c]

    def ag_ahead(c):
        for b in range(2):
            ag_z(half(zh, c, b), 1 - 2 * c, 3 * c + b).start()

    pltpu.make_async_copy(kv.at[:, zh, y, core], kv.at[:, zh, y, core], loc.at[1]).wait()
    for c in range(2):
        pl.when(core == c)(lambda c=c: ag_ahead(c))
    got(sub(zh, y, other), sib_r.at[0])
    for c in range(2):
        pl.when(core != c)(lambda c=c: ag_ahead(c))
    ag_z(sub(zh, y, 1), 1, 2).start()
    ag_z(sub(zh, y, 0), -1, 5).start()
    ag_send_y(kv.at[:, zh, y], 0)

    for c in local[5:]:
        c.wait()
    got(gb.at[pl.ds(pl.multiple_of(other * ROWS, ROWS), ROWS), :], sib_r.at[1])
    got(q2.at[pl.ds(pl.multiple_of(other * ROWS, ROWS), ROWS), :], sib_r.at[2])
    dat[...] = nt(w_v[...], gb[...]).astype(BF)
    da[...] = nt(gb[...], w_v[...]).astype(BF)
    prepare(0)
    prepare(1)

    for b in range(2):
        for z, c, way in ((z3, 0, 1), (z1, 1, -1)):
            got(half(z, c, b), agz_r.at[3 * c + b])
            ag_z(half(z, c, b), way, 6 + 2 * c + b).start()
            ag_send_y(half(z, c, b), 1 + c)
    for z, c in ((z3, 1), (z1, 0)):
        got(sub(z, y, c), agz_r.at[2 + 3 * (1 - c)])
        ag_send_y(sub(z, y, c), 2 - c)
    for b in range(2):
        for c in range(2):
            got(half(z2, c, b), agz_r.at[6 + 2 * c + b])
        ag_send_y(kv.at[b, z2, y], 3 + b)

    def keys_of(b, z):
        return kv[b, z, :, :, 0].reshape(256, 128)

    def values_of(b, z):
        return kv[b, z, :, :, 1].reshape(256, 128)

    def all_of(b, t):
        return kv[b, :, :, :, t].reshape(1024, 128)

    order = (zh, z3, z1, z2)
    tops, totals, gains = ([[None] * 2 for _ in range(4)] for _ in range(3))

    def score(i, b):
        sc = nn(keys_of(b, order[i]), qbd[b])
        top = jnp.max(sc, axis=0, keepdims=True)
        e = jnp.exp2((sc - top) * (SCALE * LOG2E))
        s_ref[b, i] = e
        tops[i][b] = top
        totals[i][b] = jnp.sum(e, axis=0, keepdims=True)
        a = tn(values_of(b, order[i]), e.astype(BF))
        ap[b, i, 0:64, :] = a[0:64, 0:256]
        ap[b, i, 64:128, :] = a[64:128, 256:512]

    def combine(b):
        top = tops[0][b]
        for i in range(1, 4):
            top = jnp.maximum(top, tops[i][b])
        f = [jnp.exp2((tops[i][b] - top) * (SCALE * LOG2E)) for i in range(4)]
        total = f[0] * totals[0][b]
        for i in range(1, 4):
            total = total + f[i] * totals[i][b]
        inv = 1.0 / total
        for i in range(4):
            gains[i][b] = f[i] * inv
        for h in range(2):
            a = None
            for i in range(4):
                part = ap[b, i, h * 64 : h * 64 + 64, :] * gains[i][b][:, h * 256 : h * 256 + 256]
                a = part if a is None else a + part
            at[b * 128 + h * 64 : b * 128 + h * 64 + 64, :] = a.astype(BF)

    def delta_of(b):
        cols = slice(b * 128, b * 128 + 128)
        prod = dat[cols, :].astype(F32) * at[cols, :].astype(F32)
        return jnp.concatenate(
            [jnp.sum(prod[0:64], axis=0, keepdims=True), jnp.sum(prod[64:128], axis=0, keepdims=True)], axis=1
        )

    def backward(i, b, delta):
        z = order[i]
        rows = pl.ds(pl.multiple_of(z * 256, 256), 256)
        p = s_ref[b, i] * gains[i][b]
        dp = nn(values_of(b, z), dbd[b])
        ds = (p * (dp - delta)).astype(BF)
        ds_ref[b, rows] = ds
        dkv[b, z, :, :, 0] = (nn(ds, qst[b]) * SCALE).astype(BF).reshape(4, 2, LAT, 128)
        dkv[b, z, :, :, 1] = nn(p.astype(BF), dst[b]).astype(BF).reshape(4, 2, LAT, 128)

    def query_part(b):
        a = tn(all_of(b, 0), ds_ref[b]) * SCALE
        for c in range(2):
            rows = slice(c * 128, c * 128 + 128)
            dqs[b, c] = jnp.concatenate([a[0:64, rows], a[64:128, 256 + c * 128 : 384 + c * 128]], axis=0).T
        keep(dqs.at[b, core], dq_out.at[:, block_cols(core, b)])
        send(dqs.at[b, other], dq_out.at[:, block_cols(core, b)], dq_s, dq_r, sib, False)

    def add(*parts):
        out = parts[0].astype(F32)
        for p in parts[1:]:
            out = out + p.astype(F32)
        return out

    def rs_y(i):
        for k in RING:
            peer = after(y, k)
            send(dkv.at[:, order[i], peer], ry.at[i, y], ry_s, ry_r.at[i], y_peer(peer), False)

    def rs_y_far(b):
        for k in RING:
            peer = after(y, k)
            send(dkv.at[b, z2, peer], ry.at[3, y, b], ry_s, ry_r.at[3 + b], y_peer(peer), False)

    def y_sum(i):
        got(ry.at[i, 0:3], ry_r.at[i])
        red[:, order[i]] = add(dkv[:, order[i], y], ry[i, y1], ry[i, y3], ry[i, y2]).astype(BF)

    def z_send(src, dst, i, k):
        send(src, dst, rz_s.at[i, k], rz_r.at[i, k], to_z[1 - 2 * i])

    def z_final(src, dst, c, i, k):
        send(src, dst, rz_s.at[i, k], rf_r.at[i], to_z_core(1 - 2 * i, c))

    def rs_z_far(b):
        got(ry.at[3, 0:3, b], ry_r.at[3 + b])
        red[b, z2] = add(dkv[b, z2, y], ry[3, y1, b], ry[3, y3, b], ry[3, y2, b]).astype(BF)
        for c in range(2):
            z_send(red.at[b, z2, c], rz.at[c, 0, b], c, b)

    def rs_z_near():
        for i, z, c in ((2, z1, 0), (1, z3, 1)):
            y_sum(i)
            z_final(red.at[:, z, 1 - c], rzf.at[c, core], 1 - c, c, 2)

    def rs_z_last(b):
        for c, z in enumerate((z1, z3)):
            got(rz.at[c, 0, b], rz_r.at[c, b])
            red[b, z, c] = add(red[b, z, c], rz[c, 0, b]).astype(BF)
            z_final(red.at[b, z, c], rzf.at[c, core, b], c, c, 3 + b)

    def rs_pair():
        y_sum(0)
        send(red.at[:, zh, other], own.at[core], fin_s, fin_r, sib, False)
        own[core] = red[:, zh, core]

    def rs_end():
        got(own.at[other], fin_r)
        for i in range(2):
            got(rzf.at[i], rf_r.at[i])
        for h in range(2):
            part = add(own[h], rzf[0, h], rzf[1, h])
            for b in range(2):
                cols = slice(h * HALF + b * 128, h * HALF + b * 128 + 128)
                fin[0, :, cols] = part[b, 0]
                fin[1, :, cols] = part[b, 1]
        keep(fin.at[0], dk_out)
        keep(fin.at[1], dv_out)

    def rs_got():
        got(dq_out.at[:, theirs], dq_r)

    def w_start(b):
        rows = slice(b * 128, b * 128 + 128)
        wpart[b * 8 : b * 8 + 8] = nn(at[rows, :], gb[...]).astype(BF).reshape(8, 16, D)
        for k in (2, 1, 3, 0):
            for px in (2 * b, 2 * b + 1):
                peer = px * 4 + after(y, k)
                dev = (zl * 4 + px, zh * 8 + after(y, k) * 2 + core)
                c = remote(wpart.at[peer], w_a.at[plane], a_s, a_r, dev)
                if k == 0:
                    pl.when(px != x)(c.start)
                else:
                    c.start()

    def w_to_line():
        w_a[plane] = wpart[plane]
        got(w_a.at[0:15], a_r)
        total = jnp.sum(w_a[...].astype(F32), axis=0)
        for p in range(4):
            w_b_src[p] = total[:, p * 128 : p * 128 + 128].astype(BF)
        for k in LINE:
            peer = lax.rem(line + k, 16)
            send(w_b_src.at[lax.rem(peer, 4)], w_b.at[line], b_s, b_r, line_peer(peer), False)
        w_b[line] = w_b_src[zl]

    def w_to_near():
        got(w_b.at[0:15], b_r)
        w_c[zl] = (jnp.sum(w_b[...].astype(F32), axis=0) * (1.0 / SHAPES)).astype(BF)
        for k in (2, 1, 15):
            send(w_c.at[zl], w_c.at[zl], c_s, c_r, line_peer(lax.rem(line + k, 16)), False)

    def w_back():
        got(w_c.at[0:3], c_r)
        for p in range(4):
            w_d[plane, :, p * 128 : p * 128 + 128] = w_c[p]
        for d in PLANE:
            send(w_d.at[plane], w_d.at[plane], d_s, d_r, plane_peer(d), False)

    def w_pair():
        got(w_d.at[0:15], d_r)
        send(w_d, dw_out.at[core], e_s, e_r, sib)
        keep(w_d, dw_out.at[core])

    def back(i):
        for b in range(2):
            backward(i, b, deltas[b])

    for i in range(3):
        got(kv.at[:, order[i], 0:3], agy_r.at[i])
        score(i, 0)
        score(i, 1)
    for b in range(2):
        got(kv.at[b, z2, 0:3], agy_r.at[3 + b])
        score(3, b)
        combine(b)
        w_start(b)
    deltas = (delta_of(0), delta_of(1))
    for b in range(2):
        backward(3, b, deltas[b])
        rs_y_far(b)
    for i in (2, 1, 0):
        back(i)
    query_part(0)
    query_part(1)
    for i in (2, 1, 0):
        rs_y(i)
    w_to_line()
    rs_z_far(0)
    rs_z_far(1)
    w_to_near()
    rs_z_near()
    rs_z_last(0)
    rs_z_last(1)
    w_back()
    rs_pair()
    w_pair()
    rs_end()
    rs_got()
    got(dw_out.at[other], e_r)

    sent(sub(zh, y, other), sib_s.at[0])
    sent(kv.at[:, 0, 0:3], agz_s)
    sent(kv.at[:, 0:3], agy_s)
    sent(dkv.at[:, 0:3], ry_s)
    sent(own.at[0], fin_s)
    sent(dqs.at[:, 0], dq_s)
    sent(w_a.at[0:15], a_s)
    sent(w_b.at[0:15], b_s)
    sent(w_c.at[0:3], c_s)
    sent(w_d.at[0:15], d_s)
    for c in kept:
        c.wait()
    for c in sends:
        c.wait_send()


def finish(dq, dk, dv, dw, dq_out, dk_out, dv_out, dw_out, vq, vk, vv, half, full, sem):
    rest = ((dq, vq, dq_out), (dk, vk, dk_out), (dv, vv, dv_out))
    loads = [pltpu.make_async_copy(dw.at[pl.ds(i * 128, 128)], half.at[i], sem.at[i]) for i in range(4)]
    loads += [pltpu.make_async_copy(src, mid, sem.at[4 + i]) for i, (src, mid, _) in enumerate(rest)]
    stores = [pltpu.make_async_copy(full.at[i], dw_out.at[pl.ds(i * 128, 128)], sem.at[7 + i]) for i in range(4)]
    stores += [pltpu.make_async_copy(mid, dst, sem.at[11 + i]) for i, (_, mid, dst) in enumerate(rest)]
    for c in loads:
        c.start()
    for i in range(7):
        loads[i].wait()
        if i < 4:
            full[i] = half[i].astype(F32)
        stores[i].start()
    for c in stores:
        c.wait()


def shards(queries, keys, values, out_weight, out_grad):
    dma = pltpu.SemaphoreType.DMA
    vm = pltpu.VMEM
    one = pl.BlockSpec(memory_space=pltpu.HBM)
    sizes = ((ROWS, D), (LAT, D), (LAT, D))
    dq, dk, dv, dw = pl.pallas_call(
        kernel,
        out_shape=[jax.ShapeDtypeStruct(i, F32) for i in sizes] + [jax.ShapeDtypeStruct((2, 16, 16, D), BF)],
        in_specs=[one] * 5,
        out_specs=[one] * 4,
        scratch_shapes=[
            vm((2, 4, 4, 2, 2, LAT, 128), BF),
            vm((256, 256), BF),
            vm((256, D), BF),
            vm((ROWS, D), F32),
            vm((256, D), BF),
            vm((256, 256), BF),
            vm((256, 256), BF),
            vm((2, 4, 256, 512), F32),
            vm((2, 4, 128, 256), F32),
            vm((2, 1024, 512), BF),
            vm((256, 256), BF),
            vm((2, 128, 512), BF),
            vm((2, 128, 512), BF),
            vm((2, 512, 128), BF),
            vm((2, 512, 128), BF),
            vm((2, 4, 4, 2, 2, LAT, 128), BF),
            vm((4, 4, 2, 2, 2, LAT, 128), BF),
            vm((2, 1, 2, 2, LAT, 128), BF),
            vm((2, 2, 2, 2, LAT, 128), BF),
            vm((2, 2, 2, LAT, 128), BF),
            vm((2, 4, 2, 2, LAT, 128), BF),
            vm((2, LAT, D), F32),
            vm((2, 2, 128, 128), F32),
            vm((16, 16, D), BF),
            vm((16, 16, D), BF),
            vm((4, 16, 128), BF),
            vm((16, 16, 128), BF),
            vm((4, 16, 128), BF),
            vm((16, 16, D), BF),
            dma((11,)), dma((3,)), dma((3,)),
            dma, dma((10,)), dma, dma((5,)),
            dma, dma((5,)), dma((2, 5)), dma((2, 2)), dma((2,)),
            dma, dma, dma, dma,
            dma, dma, dma, dma, dma, dma, dma, dma, dma, dma,
        ],
        compiler_params=pltpu.CompilerParams(
            collective_id=0, has_side_effects=True, vmem_limit_bytes=58 * 1024 * 1024
        ),
        name="attend_back",
    )(queries[0], keys[0], values[0], out_weight, out_grad[0])
    dq, dk, dv, dw = pl.pallas_call(
        finish,
        out_shape=[jax.ShapeDtypeStruct(i, F32) for i in sizes + ((D, D),)],
        in_specs=[one] * 4,
        out_specs=[one] * 4,
        scratch_shapes=[vm(i, F32) for i in sizes] + [vm((4, 128, D), BF), vm((4, 128, D), F32), dma((14,))],
        compiler_params=pltpu.CompilerParams(vmem_limit_bytes=58 * 1024 * 1024),
        name="finish",
    )(dq, dk, dv, dw.reshape(D, D))
    return (dq[None], dk[None], dv[None], dw)


def solution(mesh):
    part = P("shape", "query", None)
    return jax.shard_map(
        shards,
        mesh=mesh,
        in_specs=(part, part, part, P(), part),
        out_specs=(part, part, part, P()),
        check_vma=False,
    )
```

```python
import math

import jax
import jax.numpy as jnp
from jax import lax
from jax.experimental import pallas as pl
from jax.experimental.pallas import tpu as pltpu
from jax.sharding import PartitionSpec as P

MESH = pl.DeviceIdType.MESH
BF = jnp.bfloat16
F32 = jnp.float32

ROWS = 128
LAT = 32
D = 512
HALF = 256
SHAPES = 16
SCALE = 1.0 / math.sqrt(64)
LOG2E = 1.4426950408889634
RING = (2, 1, 3)
PLANE = ((2, 2), (2, 1), (2, 3), (1, 2), (3, 2), (2, 0), (0, 2), (1, 1), (1, 3), (3, 1), (3, 3), (1, 0), (3, 0), (0, 1), (0, 3))
LINE = (8, 7, 9, 6, 10, 5, 11, 4, 12, 3, 13, 2, 14, 1, 15)


def nt(a, b):
    return lax.dot_general(a, b, (((1,), (1,)), ((), ())), preferred_element_type=F32)


def tn(a, b):
    return lax.dot_general(a, b, (((0,), (0,)), ((), ())), preferred_element_type=F32)


def nn(a, b):
    return lax.dot_general(a, b, (((1,), (0,)), ((), ())), preferred_element_type=F32)


def kernel(
    q_hbm, k_hbm, v_hbm, w_hbm, g_hbm,
    dq_out, dk_out, dv_out, dw_out,
    kv, q2, gb, gst, w_v, dat, da, s_ref, ap, ds_ref, at, qbd, dbd, qst, dst,
    dkv, ry, rz, rzf, own, red, fin, dqs, wpart, w_a, w_b_src, w_b, w_c, w_d,
    loc, sib_s, sib_r, agz_s, agz_r, agy_s, agy_r, ry_s, ry_r, rz_s, rz_r, rf_r, fin_s, fin_r, dq_s, dq_r,
    a_s, a_r, b_s, b_r, c_s, c_r, d_s, d_r, e_s, e_r,
):
    shape_at = lax.axis_index("shape")
    query_at = lax.axis_index("query")
    core = lax.rem(query_at, 2)
    other = 1 - core
    y = lax.rem(lax.div(query_at, 2), 4)
    zh = lax.div(query_at, 8)
    x = lax.rem(shape_at, 4)
    zl = lax.div(shape_at, 4)
    y1, y2, y3 = [lax.rem(y + i, 4) for i in (1, 2, 3)]
    z1, z2, z3 = [lax.rem(zh + i, 4) for i in (1, 2, 3)]
    sib = (shape_at, query_at + 1 - 2 * core)
    to_z = {1: (shape_at, z1 * 8 + y * 2 + core), -1: (shape_at, z3 * 8 + y * 2 + core)}
    def to_z_core(way, c):
        return (shape_at, (z1 if way == 1 else z3) * 8 + y * 2 + c)

    to_y = {1: (shape_at, zh * 8 + y1 * 2 + core), -1: (shape_at, zh * 8 + y3 * 2 + core)}
    def after(i, k):
        return lax.rem(i + k, 4)

    line = zh * 4 + zl
    plane = x * 4 + y

    def y_peer(i):
        return (shape_at, zh * 8 + i * 2 + core)

    def plane_at(d):
        return after(x, d[0]) * 4 + after(y, d[1])

    def plane_peer(d):
        return (zl * 4 + after(x, d[0]), zh * 8 + after(y, d[1]) * 2 + core)

    def line_peer(i):
        return (lax.rem(i, 4) * 4 + x, lax.div(i, 4) * 8 + y * 2 + core)

    barrier = pltpu.get_barrier_semaphore()

    def greet(dev):
        pl.semaphore_signal(barrier, inc=1, device_id=dev, device_id_type=MESH)

    greet(to_z[1])
    greet(to_z[-1])
    for k in (1, 2, 3):
        greet(line_peer(zh * 4 + after(zl, k)))

    for d in PLANE:
        greet(plane_peer(d))
    greet(sib)

    mine = pl.ds(pl.multiple_of(core * HALF, HALF), HALF)
    theirs = pl.ds(pl.multiple_of(other * HALF, HALF), HALF)
    my_rows = pl.ds(pl.multiple_of(core * ROWS, ROWS), ROWS)

    def block_cols(c, b):
        return pl.ds(pl.multiple_of(c * HALF + b * 128, 128), 128)

    local = [pltpu.make_async_copy(g_hbm, gst, loc.at[0])]
    for b in range(2):
        for t, ref in enumerate((k_hbm, v_hbm)):
            local.append(
                pltpu.make_async_copy(ref.at[:, block_cols(core, b)], kv.at[b, zh, y, core, t], loc.at[1])
            )
    local.append(pltpu.make_async_copy(w_hbm.at[mine, :], w_v, loc.at[2]))
    local.append(pltpu.make_async_copy(q_hbm.at[:, mine], q2.at[my_rows, :], loc.at[3]))
    for c in local:
        c.start()
    local[0].wait()
    gb[my_rows, :] = gst[...].astype(BF)

    sends = []
    kept = []

    def keep(src, dst):
        c = pltpu.make_async_copy(src, dst, loc.at[4 + len(kept)])
        c.start()
        kept.append(c)

    def remote(src, dst, ss, rs, dev):
        return pltpu.make_async_remote_copy(
            src_ref=src, dst_ref=dst, send_sem=ss, recv_sem=rs, device_id=dev, device_id_type=MESH
        )

    def send(src, dst, ss, rs, dev, wait=True):
        c = remote(src, dst, ss, rs, dev)
        c.start()
        if wait:
            sends.append(c)

    def got(ref, sem):
        remote(ref, ref, sem, sem, sib).wait_recv()

    def sent(ref, sem):
        remote(ref, ref, sem, sem, sib).wait_send()

    pl.semaphore_wait(barrier, 21)

    for b in range(2):
        for t, ref in enumerate((k_hbm, v_hbm)):
            send(ref.at[:, block_cols(other, b)], kv.at[b, zh, y, core, t], sib_s.at[0], sib_r.at[0], sib, False)
    send(gb.at[my_rows, :], gb.at[my_rows, :], sib_s.at[1], sib_r.at[1], sib)
    send(q_hbm.at[:, theirs], q2.at[my_rows, :], sib_s.at[2], sib_r.at[2], sib)

    low = lax.broadcasted_iota(jnp.int32, (256, 128), 1) < 64
    zero = jnp.zeros((64, 256), BF)

    def prepare(b):
        cols = slice(b * 128, b * 128 + 128)
        q_t = q2[:, cols].T
        for ref, part in ((qbd, q_t), (dbd, dat[cols, :])):
            ref[b, 0:64, 0:256] = part[0:64]
            ref[b, 0:64, 256:512] = zero
            ref[b, 64:128, 0:256] = zero
            ref[b, 64:128, 256:512] = part[64:128]
        none = jnp.zeros((256, 128), BF)
        for ref, part in ((qst, q2[:, cols]), (dst, da[:, cols])):
            ref[b, 0:256] = jnp.where(low, part, none)
            ref[b, 256:512] = jnp.where(low, none, part)

    def sub(z, yy, c):
        return kv.at[:, z, yy, c]

    def ag_z(ref, way, sem):
        return remote(ref, ref, agz_s, agz_r.at[sem], to_z[way])

    def ag_send_y(ref, sem):
        for k in RING:
            send(ref, ref, agy_s, agy_r.at[sem], y_peer(after(y, k)), False)

    def half(z, c, b):
        return kv.at[b, z, y, c]

    def ag_ahead(c):
        for b in range(2):
            ag_z(half(zh, c, b), 1 - 2 * c, 3 * c + b).start()

    pltpu.make_async_copy(kv.at[:, zh, y, core], kv.at[:, zh, y, core], loc.at[1]).wait()
    for c in range(2):
        pl.when(core == c)(lambda c=c: ag_ahead(c))
    got(sub(zh, y, other), sib_r.at[0])
    for c in range(2):
        pl.when(core != c)(lambda c=c: ag_ahead(c))
    ag_z(sub(zh, y, 1), 1, 2).start()
    ag_z(sub(zh, y, 0), -1, 5).start()
    ag_send_y(kv.at[:, zh, y], 0)

    for c in local[5:]:
        c.wait()
    got(gb.at[pl.ds(pl.multiple_of(other * ROWS, ROWS), ROWS), :], sib_r.at[1])
    got(q2.at[pl.ds(pl.multiple_of(other * ROWS, ROWS), ROWS), :], sib_r.at[2])
    dat[...] = nt(w_v[...], gb[...]).astype(BF)
    da[...] = nt(gb[...], w_v[...]).astype(BF)
    prepare(0)
    prepare(1)

    for b in range(2):
        for z, c, way in ((z3, 0, 1), (z1, 1, -1)):
            got(half(z, c, b), agz_r.at[3 * c + b])
            ag_z(half(z, c, b), way, 6 + 2 * c + b).start()
            ag_send_y(half(z, c, b), 1 + c)
    for z, c in ((z3, 1), (z1, 0)):
        got(sub(z, y, c), agz_r.at[2 + 3 * (1 - c)])
        ag_send_y(sub(z, y, c), 2 - c)
    for b in range(2):
        for c in range(2):
            got(half(z2, c, b), agz_r.at[6 + 2 * c + b])
        ag_send_y(kv.at[b, z2, y], 3 + b)

    def keys_of(b, z):
        return kv[b, z, :, :, 0].reshape(256, 128)

    def values_of(b, z):
        return kv[b, z, :, :, 1].reshape(256, 128)

    def all_of(b, t):
        return kv[b, :, :, :, t].reshape(1024, 128)

    order = (zh, z3, z1, z2)
    tops, totals, gains = ([[None] * 2 for _ in range(4)] for _ in range(3))

    def score(i, b):
        sc = nn(keys_of(b, order[i]), qbd[b])
        top = jnp.max(sc, axis=0, keepdims=True)
        e = jnp.exp2((sc - top) * (SCALE * LOG2E))
        s_ref[b, i] = e
        tops[i][b] = top
        totals[i][b] = jnp.sum(e, axis=0, keepdims=True)
        a = tn(values_of(b, order[i]), e.astype(BF))
        ap[b, i, 0:64, :] = a[0:64, 0:256]
        ap[b, i, 64:128, :] = a[64:128, 256:512]

    def joined(b, blocks):
        top = tops[blocks[0]][b]
        for i in blocks[1:]:
            top = jnp.maximum(top, tops[i][b])
        f = [jnp.exp2((tops[i][b] - top) * (SCALE * LOG2E)) for i in blocks]
        total = f[0] * totals[blocks[0]][b]
        for i, g in zip(blocks[1:], f[1:]):
            total = total + g * totals[i][b]
        return top, f, total

    def weigh(b, blocks, f, h):
        a = None
        for i, g in zip(blocks, f):
            part = ap[b, i, h * 64 : h * 64 + 64, :] * g[:, h * 256 : h * 256 + 256]
            a = part if a is None else a + part
        return a

    def early(b):
        top, f, total = joined(b, (0, 1, 2))
        for h in range(2):
            ap[b, 0, h * 64 : h * 64 + 64, :] = weigh(b, (0, 1, 2), f, h)
        tops[0][b], totals[0][b] = top, total
        for i in range(3):
            gains[i][b] = f[i]

    def combine(b):
        _, f, total = joined(b, (0, 3))
        inv = 1.0 / total
        f = [g * inv for g in f]
        for i in range(3):
            gains[i][b] = gains[i][b] * f[0]
        gains[3][b] = f[1]
        for h in range(2):
            at[b * 128 + h * 64 : b * 128 + h * 64 + 64, :] = weigh(b, (0, 3), f, h).astype(BF)

    def delta_of(b):
        cols = slice(b * 128, b * 128 + 128)
        prod = dat[cols, :].astype(F32) * at[cols, :].astype(F32)
        return jnp.concatenate(
            [jnp.sum(prod[0:64], axis=0, keepdims=True), jnp.sum(prod[64:128], axis=0, keepdims=True)], axis=1
        )

    def backward(i, b, delta):
        z = order[i]
        rows = pl.ds(pl.multiple_of(z * 256, 256), 256)
        p = s_ref[b, i] * gains[i][b]
        dp = nn(values_of(b, z), dbd[b])
        ds = (p * (dp - delta)).astype(BF)
        ds_ref[b, rows] = ds
        dkv[b, z, :, :, 0] = (nn(ds, qst[b]) * SCALE).astype(BF).reshape(4, 2, LAT, 128)
        dkv[b, z, :, :, 1] = nn(p.astype(BF), dst[b]).astype(BF).reshape(4, 2, LAT, 128)

    def query_part(b):
        a = tn(all_of(b, 0), ds_ref[b]) * SCALE
        for c in range(2):
            rows = slice(c * 128, c * 128 + 128)
            dqs[b, c] = jnp.concatenate([a[0:64, rows], a[64:128, 256 + c * 128 : 384 + c * 128]], axis=0).T
        keep(dqs.at[b, core], dq_out.at[:, block_cols(core, b)])
        send(dqs.at[b, other], dq_out.at[:, block_cols(core, b)], dq_s, dq_r, sib, False)

    def add(*parts):
        out = parts[0].astype(F32)
        for p in parts[1:]:
            out = out + p.astype(F32)
        return out

    def rs_y(i):
        for k in RING:
            peer = after(y, k)
            send(dkv.at[:, order[i], peer], ry.at[i, y], ry_s, ry_r.at[i], y_peer(peer), False)

    def rs_y_far(b):
        for k in RING:
            peer = after(y, k)
            send(dkv.at[b, z2, peer], ry.at[3, y, b], ry_s, ry_r.at[3 + b], y_peer(peer), False)

    def y_sum(i):
        got(ry.at[i, 0:3], ry_r.at[i])
        red[:, order[i]] = add(dkv[:, order[i], y], ry[i, y1], ry[i, y3], ry[i, y2]).astype(BF)

    def z_send(src, dst, i, k):
        send(src, dst, rz_s.at[i, k], rz_r.at[i, k], to_z[1 - 2 * i])

    def z_final(src, dst, c, i, k):
        send(src, dst, rz_s.at[i, k], rf_r.at[i], to_z_core(1 - 2 * i, c))

    def rs_z_far(b):
        got(ry.at[3, 0:3, b], ry_r.at[3 + b])
        red[b, z2] = add(dkv[b, z2, y], ry[3, y1, b], ry[3, y3, b], ry[3, y2, b]).astype(BF)
        for c in range(2):
            z_send(red.at[b, z2, c], rz.at[c, 0, b], c, b)

    def rs_z_near():
        for i, z, c in ((2, z1, 0), (1, z3, 1)):
            y_sum(i)
            z_final(red.at[:, z, 1 - c], rzf.at[c, core], 1 - c, c, 2)

    def rs_z_last(b):
        for c, z in enumerate((z1, z3)):
            got(rz.at[c, 0, b], rz_r.at[c, b])
            red[b, z, c] = add(red[b, z, c], rz[c, 0, b]).astype(BF)
            z_final(red.at[b, z, c], rzf.at[c, core, b], c, c, 3 + b)

    def rs_pair():
        y_sum(0)
        send(red.at[:, zh, other], own.at[core], fin_s, fin_r, sib, False)
        own[core] = red[:, zh, core]

    def rs_end():
        got(own.at[other], fin_r)
        for i in range(2):
            got(rzf.at[i], rf_r.at[i])
        for h in range(2):
            part = add(own[h], rzf[0, h], rzf[1, h])
            for b in range(2):
                cols = slice(h * HALF + b * 128, h * HALF + b * 128 + 128)
                fin[0, :, cols] = part[b, 0]
                fin[1, :, cols] = part[b, 1]
        keep(fin.at[0], dk_out)
        keep(fin.at[1], dv_out)

    def rs_got():
        got(dq_out.at[:, theirs], dq_r)

    def w_start(b):
        rows = slice(b * 128, b * 128 + 128)
        wpart[b * 8 : b * 8 + 8] = nn(at[rows, :], gb[...]).astype(BF).reshape(8, 16, D)
        for k in (2, 1, 3, 0):
            for px in (2 * b, 2 * b + 1):
                peer = px * 4 + after(y, k)
                dev = (zl * 4 + px, zh * 8 + after(y, k) * 2 + core)
                c = remote(wpart.at[peer], w_a.at[plane], a_s, a_r, dev)
                if k == 0:
                    pl.when(px != x)(c.start)
                else:
                    c.start()

    def w_to_line():
        w_a[plane] = wpart[plane]
        got(w_a.at[0:15], a_r)
        total = jnp.sum(w_a[...].astype(F32), axis=0)
        for p in range(4):
            w_b_src[p] = total[:, p * 128 : p * 128 + 128].astype(BF)
        for k in LINE:
            peer = lax.rem(line + k, 16)
            send(w_b_src.at[lax.rem(peer, 4)], w_b.at[line], b_s, b_r, line_peer(peer), False)
        w_b[line] = w_b_src[zl]

    def w_to_near():
        got(w_b.at[0:15], b_r)
        w_c[zl] = (jnp.sum(w_b[...].astype(F32), axis=0) * (1.0 / SHAPES)).astype(BF)
        for k in (2, 1, 15):
            send(w_c.at[zl], w_c.at[zl], c_s, c_r, line_peer(lax.rem(line + k, 16)), False)

    def w_back():
        got(w_c.at[0:3], c_r)
        for p in range(4):
            w_d[plane, :, p * 128 : p * 128 + 128] = w_c[p]
        for d in PLANE:
            send(w_d.at[plane], w_d.at[plane], d_s, d_r, plane_peer(d), False)

    def w_pair():
        got(w_d.at[0:15], d_r)
        send(w_d, dw_out.at[core], e_s, e_r, sib)
        keep(w_d, dw_out.at[core])

    def back(i):
        for b in range(2):
            backward(i, b, deltas[b])
        rs_y(i)

    for i in range(3):
        got(kv.at[:, order[i], 0:3], agy_r.at[i])
        score(i, 0)
        score(i, 1)
    early(0)
    early(1)
    for b in range(2):
        got(kv.at[b, z2, 0:3], agy_r.at[3 + b])
        score(3, b)
        combine(b)
        w_start(b)
    deltas = (delta_of(0), delta_of(1))
    for b in range(2):
        backward(3, b, deltas[b])
        rs_y_far(b)
    for i in (2, 1, 0):
        back(i)
    query_part(0)
    query_part(1)
    w_to_line()
    rs_z_far(0)
    rs_z_far(1)
    w_to_near()
    rs_z_near()
    rs_z_last(0)
    rs_z_last(1)
    w_back()
    rs_pair()
    w_pair()
    rs_end()
    rs_got()
    got(dw_out.at[other], e_r)

    sent(sub(zh, y, other), sib_s.at[0])
    sent(kv.at[:, 0, 0:3], agz_s)
    sent(kv.at[:, 0:3], agy_s)
    sent(dkv.at[:, 0:3], ry_s)
    sent(own.at[0], fin_s)
    sent(dqs.at[:, 0], dq_s)
    sent(w_a.at[0:15], a_s)
    sent(w_b.at[0:15], b_s)
    sent(w_c.at[0:3], c_s)
    sent(w_d.at[0:15], d_s)
    for c in kept:
        c.wait()
    for c in sends:
        c.wait_send()


def finish(dq, dk, dv, dw, dq_out, dk_out, dv_out, dw_out, vq, vk, vv, half, full, sem):
    rest = ((dq, vq, dq_out), (dk, vk, dk_out), (dv, vv, dv_out))
    loads = [pltpu.make_async_copy(dw.at[pl.ds(i * 128, 128)], half.at[i], sem.at[i]) for i in range(4)]
    loads += [pltpu.make_async_copy(src, mid, sem.at[4 + i]) for i, (src, mid, _) in enumerate(rest)]
    stores = [pltpu.make_async_copy(full.at[i], dw_out.at[pl.ds(i * 128, 128)], sem.at[7 + i]) for i in range(4)]
    stores += [pltpu.make_async_copy(mid, dst, sem.at[11 + i]) for i, (_, mid, dst) in enumerate(rest)]
    for c in loads:
        c.start()
    for i in range(7):
        loads[i].wait()
        if i < 4:
            full[i] = half[i].astype(F32)
        stores[i].start()
    for c in stores:
        c.wait()


def shards(queries, keys, values, out_weight, out_grad):
    dma = pltpu.SemaphoreType.DMA
    vm = pltpu.VMEM
    one = pl.BlockSpec(memory_space=pltpu.HBM)
    sizes = ((ROWS, D), (LAT, D), (LAT, D))
    dq, dk, dv, dw = pl.pallas_call(
        kernel,
        out_shape=[jax.ShapeDtypeStruct(i, F32) for i in sizes] + [jax.ShapeDtypeStruct((2, 16, 16, D), BF)],
        in_specs=[one] * 5,
        out_specs=[one] * 4,
        scratch_shapes=[
            vm((2, 4, 4, 2, 2, LAT, 128), BF),
            vm((256, 256), BF),
            vm((256, D), BF),
            vm((ROWS, D), F32),
            vm((256, D), BF),
            vm((256, 256), BF),
            vm((256, 256), BF),
            vm((2, 4, 256, 512), F32),
            vm((2, 4, 128, 256), F32),
            vm((2, 1024, 512), BF),
            vm((256, 256), BF),
            vm((2, 128, 512), BF),
            vm((2, 128, 512), BF),
            vm((2, 512, 128), BF),
            vm((2, 512, 128), BF),
            vm((2, 4, 4, 2, 2, LAT, 128), BF),
            vm((4, 4, 2, 2, 2, LAT, 128), BF),
            vm((2, 1, 2, 2, LAT, 128), BF),
            vm((2, 2, 2, 2, LAT, 128), BF),
            vm((2, 2, 2, LAT, 128), BF),
            vm((2, 4, 2, 2, LAT, 128), BF),
            vm((2, LAT, D), F32),
            vm((2, 2, 128, 128), F32),
            vm((16, 16, D), BF),
            vm((16, 16, D), BF),
            vm((4, 16, 128), BF),
            vm((16, 16, 128), BF),
            vm((4, 16, 128), BF),
            vm((16, 16, D), BF),
            dma((11,)), dma((3,)), dma((3,)),
            dma, dma((10,)), dma, dma((5,)),
            dma, dma((5,)), dma((2, 5)), dma((2, 2)), dma((2,)),
            dma, dma, dma, dma,
            dma, dma, dma, dma, dma, dma, dma, dma, dma, dma,
        ],
        compiler_params=pltpu.CompilerParams(
            collective_id=0, has_side_effects=True, vmem_limit_bytes=58 * 1024 * 1024
        ),
        name="attend_back",
    )(queries[0], keys[0], values[0], out_weight, out_grad[0])
    dq, dk, dv, dw = pl.pallas_call(
        finish,
        out_shape=[jax.ShapeDtypeStruct(i, F32) for i in sizes + ((D, D),)],
        in_specs=[one] * 4,
        out_specs=[one] * 4,
        scratch_shapes=[vm(i, F32) for i in sizes] + [vm((4, 128, D), BF), vm((4, 128, D), F32), dma((14,))],
        compiler_params=pltpu.CompilerParams(vmem_limit_bytes=58 * 1024 * 1024),
        name="finish",
    )(dq, dk, dv, dw.reshape(D, D))
    return (dq[None], dk[None], dv[None], dw)


def solution(mesh):
    part = P("shape", "query", None)
    return jax.shard_map(
        shards,
        mesh=mesh,
        in_specs=(part, part, part, P(), part),
        out_specs=(part, part, part, P()),
        check_vma=False,
    )
```

```python
import math

import jax
import jax.numpy as jnp
from jax import lax
from jax.experimental import pallas as pl
from jax.experimental.pallas import tpu as pltpu
from jax.sharding import PartitionSpec as P

MESH = pl.DeviceIdType.MESH
BF = jnp.bfloat16
F32 = jnp.float32

ROWS = 128
LAT = 32
D = 512
HALF = 256
SHAPES = 16
SCALE = 1.0 / math.sqrt(64)
LOG2E = 1.4426950408889634
RING = (2, 1, 3)
PLANE = ((2, 2), (2, 1), (2, 3), (1, 2), (3, 2), (2, 0), (0, 2), (1, 1), (1, 3), (3, 1), (3, 3), (1, 0), (3, 0), (0, 1), (0, 3))
LINE = (8, 7, 9, 6, 10, 5, 11, 4, 12, 3, 13, 2, 14, 1, 15)


def nt(a, b):
    return lax.dot_general(a, b, (((1,), (1,)), ((), ())), preferred_element_type=F32)


def tn(a, b):
    return lax.dot_general(a, b, (((0,), (0,)), ((), ())), preferred_element_type=F32)


def nn(a, b):
    return lax.dot_general(a, b, (((1,), (0,)), ((), ())), preferred_element_type=F32)


def kernel(
    q_hbm, k_hbm, v_hbm, w_hbm, g_hbm,
    dq_out, dk_out, dv_out, dw_out,
    kv, q2, gb, gst, w_v, dat, da, s_ref, ap, ds_ref, at, qbd, dbd, qst, dst,
    dkv, ry, rz, rzf, own, red, fin, dqs, wpart, w_a, w_b_src, w_b, w_c, w_d,
    loc, sib_s, sib_r, agz_s, agz_r, agy_s, agy_r, ry_s, ry_r, rz_s, rz_r, rf_r, fin_s, fin_r, dq_s, dq_r,
    a_s, a_r, b_s, b_r, c_s, c_r, d_s, d_r, e_s, e_r,
):
    shape_at = lax.axis_index("shape")
    query_at = lax.axis_index("query")
    core = lax.rem(query_at, 2)
    other = 1 - core
    y = lax.rem(lax.div(query_at, 2), 4)
    zh = lax.div(query_at, 8)
    x = lax.rem(shape_at, 4)
    zl = lax.div(shape_at, 4)
    y1, y2, y3 = [lax.rem(y + i, 4) for i in (1, 2, 3)]
    z1, z2, z3 = [lax.rem(zh + i, 4) for i in (1, 2, 3)]
    sib = (shape_at, query_at + 1 - 2 * core)
    to_z = {1: (shape_at, z1 * 8 + y * 2 + core), -1: (shape_at, z3 * 8 + y * 2 + core)}
    def to_z_core(way, c):
        return (shape_at, (z1 if way == 1 else z3) * 8 + y * 2 + c)

    to_y = {1: (shape_at, zh * 8 + y1 * 2 + core), -1: (shape_at, zh * 8 + y3 * 2 + core)}
    def after(i, k):
        return lax.rem(i + k, 4)

    line = zh * 4 + zl
    plane = x * 4 + y

    def y_peer(i):
        return (shape_at, zh * 8 + i * 2 + core)

    def plane_at(d):
        return after(x, d[0]) * 4 + after(y, d[1])

    def plane_peer(d):
        return (zl * 4 + after(x, d[0]), zh * 8 + after(y, d[1]) * 2 + core)

    def line_peer(i):
        return (lax.rem(i, 4) * 4 + x, lax.div(i, 4) * 8 + y * 2 + core)

    barrier = pltpu.get_barrier_semaphore()

    def greet(dev):
        pl.semaphore_signal(barrier, inc=1, device_id=dev, device_id_type=MESH)

    greet(to_z[1])
    greet(to_z[-1])
    for k in (1, 2, 3):
        greet(line_peer(zh * 4 + after(zl, k)))

    for d in PLANE:
        greet(plane_peer(d))
    greet(sib)

    mine = pl.ds(pl.multiple_of(core * HALF, HALF), HALF)
    theirs = pl.ds(pl.multiple_of(other * HALF, HALF), HALF)
    my_rows = pl.ds(pl.multiple_of(core * ROWS, ROWS), ROWS)

    def block_cols(c, b):
        return pl.ds(pl.multiple_of(c * HALF + b * 128, 128), 128)

    local = [pltpu.make_async_copy(g_hbm, gst, loc.at[0])]
    for b in range(2):
        for t, ref in enumerate((k_hbm, v_hbm)):
            local.append(
                pltpu.make_async_copy(ref.at[:, block_cols(core, b)], kv.at[b, zh, y, core, t], loc.at[1])
            )
    local.append(pltpu.make_async_copy(w_hbm.at[mine, :], w_v, loc.at[2]))
    local.append(pltpu.make_async_copy(q_hbm.at[:, mine], q2.at[my_rows, :], loc.at[3]))
    for c in local:
        c.start()
    local[0].wait()
    gb[my_rows, :] = gst[...].astype(BF)

    sends = []
    kept = []

    def keep(src, dst):
        c = pltpu.make_async_copy(src, dst, loc.at[4 + len(kept)])
        c.start()
        kept.append(c)

    def remote(src, dst, ss, rs, dev):
        return pltpu.make_async_remote_copy(
            src_ref=src, dst_ref=dst, send_sem=ss, recv_sem=rs, device_id=dev, device_id_type=MESH
        )

    def send(src, dst, ss, rs, dev, wait=True):
        c = remote(src, dst, ss, rs, dev)
        c.start()
        if wait:
            sends.append(c)

    def got(ref, sem):
        remote(ref, ref, sem, sem, sib).wait_recv()

    def sent(ref, sem):
        remote(ref, ref, sem, sem, sib).wait_send()

    pl.semaphore_wait(barrier, 21)

    for b in range(2):
        for t, ref in enumerate((k_hbm, v_hbm)):
            send(ref.at[:, block_cols(other, b)], kv.at[b, zh, y, core, t], sib_s.at[0], sib_r.at[0], sib, False)
    send(gb.at[my_rows, :], gb.at[my_rows, :], sib_s.at[1], sib_r.at[1], sib)
    send(q_hbm.at[:, theirs], q2.at[my_rows, :], sib_s.at[2], sib_r.at[2], sib)

    low = lax.broadcasted_iota(jnp.int32, (256, 128), 1) < 64
    zero = jnp.zeros((64, 256), BF)

    def prepare(b):
        cols = slice(b * 128, b * 128 + 128)
        q_t = q2[:, cols].T
        for ref, part in ((qbd, q_t), (dbd, dat[cols, :])):
            ref[b, 0:64, 0:256] = part[0:64]
            ref[b, 0:64, 256:512] = zero
            ref[b, 64:128, 0:256] = zero
            ref[b, 64:128, 256:512] = part[64:128]
        none = jnp.zeros((256, 128), BF)
        for ref, part in ((qst, q2[:, cols]), (dst, da[:, cols])):
            ref[b, 0:256] = jnp.where(low, part, none)
            ref[b, 256:512] = jnp.where(low, none, part)

    def sub(z, yy, c):
        return kv.at[:, z, yy, c]

    def ag_z(ref, way, sem):
        return remote(ref, ref, agz_s, agz_r.at[sem], to_z[way])

    def ag_send_y(ref, sem):
        for k in RING:
            send(ref, ref, agy_s, agy_r.at[sem], y_peer(after(y, k)), False)

    def half(z, c, b):
        return kv.at[b, z, y, c]

    def ag_ahead(c):
        for b in range(2):
            ag_z(half(zh, c, b), 1 - 2 * c, 3 * c + b).start()

    pltpu.make_async_copy(kv.at[:, zh, y, core], kv.at[:, zh, y, core], loc.at[1]).wait()
    for c in range(2):
        pl.when(core == c)(lambda c=c: ag_ahead(c))
    got(sub(zh, y, other), sib_r.at[0])
    for c in range(2):
        pl.when(core != c)(lambda c=c: ag_ahead(c))
    ag_z(sub(zh, y, 1), 1, 2).start()
    ag_z(sub(zh, y, 0), -1, 5).start()
    ag_send_y(kv.at[:, zh, y], 0)

    for c in local[5:]:
        c.wait()
    got(gb.at[pl.ds(pl.multiple_of(other * ROWS, ROWS), ROWS), :], sib_r.at[1])
    got(q2.at[pl.ds(pl.multiple_of(other * ROWS, ROWS), ROWS), :], sib_r.at[2])
    dat[...] = nt(w_v[...], gb[...]).astype(BF)
    da[...] = nt(gb[...], w_v[...]).astype(BF)
    prepare(0)
    prepare(1)

    for b in range(2):
        for z, c, way in ((z3, 0, 1), (z1, 1, -1)):
            got(half(z, c, b), agz_r.at[3 * c + b])
            ag_z(half(z, c, b), way, 6 + 2 * c + b).start()
            ag_send_y(half(z, c, b), 1 + c)
    for z, c in ((z3, 1), (z1, 0)):
        got(sub(z, y, c), agz_r.at[2 + 3 * (1 - c)])
        ag_send_y(sub(z, y, c), 2 - c)
    for b in range(2):
        for c in range(2):
            got(half(z2, c, b), agz_r.at[6 + 2 * c + b])
        ag_send_y(kv.at[b, z2, y], 3 + b)

    def keys_of(b, z):
        return kv[b, z, :, :, 0].reshape(256, 128)

    def values_of(b, z):
        return kv[b, z, :, :, 1].reshape(256, 128)

    def all_of(b, t):
        return kv[b, :, :, :, t].reshape(1024, 128)

    order = (zh, z3, z1, z2)
    tops, totals, gains = ([[None] * 2 for _ in range(4)] for _ in range(3))

    def score(i, b):
        sc = nn(keys_of(b, order[i]), qbd[b])
        top = jnp.max(sc, axis=0, keepdims=True)
        e = jnp.exp2((sc - top) * (SCALE * LOG2E))
        s_ref[b, i] = e
        tops[i][b] = top
        totals[i][b] = jnp.sum(e, axis=0, keepdims=True)
        a = tn(values_of(b, order[i]), e.astype(BF))
        ap[b, i, 0:64, :] = a[0:64, 0:256]
        ap[b, i, 64:128, :] = a[64:128, 256:512]

    def combine(b):
        top = tops[0][b]
        for i in range(1, 4):
            top = jnp.maximum(top, tops[i][b])
        f = [jnp.exp2((tops[i][b] - top) * (SCALE * LOG2E)) for i in range(4)]
        total = f[0] * totals[0][b]
        for i in range(1, 4):
            total = total + f[i] * totals[i][b]
        inv = 1.0 / total
        for i in range(4):
            gains[i][b] = f[i] * inv
        for h in range(2):
            a = None
            for i in range(4):
                part = ap[b, i, h * 64 : h * 64 + 64, :] * gains[i][b][:, h * 256 : h * 256 + 256]
                a = part if a is None else a + part
            at[b * 128 + h * 64 : b * 128 + h * 64 + 64, :] = a.astype(BF)

    def delta_of(b):
        cols = slice(b * 128, b * 128 + 128)
        prod = dat[cols, :].astype(F32) * at[cols, :].astype(F32)
        return jnp.concatenate(
            [jnp.sum(prod[0:64], axis=0, keepdims=True), jnp.sum(prod[64:128], axis=0, keepdims=True)], axis=1
        )

    def backward(i, b, delta):
        z = order[i]
        rows = pl.ds(pl.multiple_of(z * 256, 256), 256)
        p = s_ref[b, i] * gains[i][b]
        dp = nn(values_of(b, z), dbd[b])
        ds = (p * (dp - delta)).astype(BF)
        ds_ref[b, rows] = ds
        dkv[b, z, :, :, 0] = (nn(ds, qst[b]) * SCALE).astype(BF).reshape(4, 2, LAT, 128)
        dkv[b, z, :, :, 1] = nn(p.astype(BF), dst[b]).astype(BF).reshape(4, 2, LAT, 128)

    def query_part(b):
        a = tn(all_of(b, 0), ds_ref[b]) * SCALE
        for c in range(2):
            rows = slice(c * 128, c * 128 + 128)
            dqs[b, c] = jnp.concatenate([a[0:64, rows], a[64:128, 256 + c * 128 : 384 + c * 128]], axis=0).T
        keep(dqs.at[b, core], dq_out.at[:, block_cols(core, b)])
        send(dqs.at[b, other], dq_out.at[:, block_cols(core, b)], dq_s, dq_r, sib, False)

    def add(*parts):
        out = parts[0].astype(F32)
        for p in parts[1:]:
            out = out + p.astype(F32)
        return out

    def rs_y(i):
        for k in RING:
            peer = after(y, k)
            send(dkv.at[:, order[i], peer], ry.at[i, y], ry_s, ry_r.at[i], y_peer(peer), False)

    def rs_y_far(b):
        for k in RING:
            peer = after(y, k)
            send(dkv.at[b, z2, peer], ry.at[3, y, b], ry_s, ry_r.at[3 + b], y_peer(peer), False)

    def y_sum(i):
        got(ry.at[i, 0:3], ry_r.at[i])
        red[:, order[i]] = add(dkv[:, order[i], y], ry[i, y1], ry[i, y3], ry[i, y2]).astype(BF)

    def z_send(src, dst, i, k):
        send(src, dst, rz_s.at[i, k], rz_r.at[i, k], to_z[1 - 2 * i])

    def z_final(src, dst, c, i, k):
        send(src, dst, rz_s.at[i, k], rf_r.at[i], to_z_core(1 - 2 * i, c))

    def rs_z_far(b):
        got(ry.at[3, 0:3, b], ry_r.at[3 + b])
        red[b, z2] = add(dkv[b, z2, y], ry[3, y1, b], ry[3, y3, b], ry[3, y2, b]).astype(BF)
        for c in range(2):
            z_send(red.at[b, z2, c], rz.at[c, 0, b], c, b)

    def rs_z_near():
        for i, z, c in ((2, z1, 0), (1, z3, 1)):
            y_sum(i)
            z_final(red.at[:, z, 1 - c], rzf.at[c, core], 1 - c, c, 2)

    def rs_z_last(b):
        for c, z in enumerate((z1, z3)):
            got(rz.at[c, 0, b], rz_r.at[c, b])
            red[b, z, c] = add(red[b, z, c], rz[c, 0, b]).astype(BF)
            z_final(red.at[b, z, c], rzf.at[c, core, b], c, c, 3 + b)

    def rs_pair():
        y_sum(0)
        send(red.at[:, zh, other], own.at[core], fin_s, fin_r, sib, False)
        own[core] = red[:, zh, core]

    def rs_end():
        got(own.at[other], fin_r)
        for i in range(2):
            got(rzf.at[i], rf_r.at[i])
        for h in range(2):
            part = add(own[h], rzf[0, h], rzf[1, h])
            for b in range(2):
                cols = slice(h * HALF + b * 128, h * HALF + b * 128 + 128)
                fin[0, :, cols] = part[b, 0]
                fin[1, :, cols] = part[b, 1]
        keep(fin.at[0], dk_out)
        keep(fin.at[1], dv_out)

    def rs_got():
        got(dq_out.at[:, theirs], dq_r)

    def w_start(b):
        rows = slice(b * 128, b * 128 + 128)
        wpart[b * 8 : b * 8 + 8] = nn(at[rows, :], gb[...]).astype(BF).reshape(8, 16, D)
        for k in (2, 1, 3, 0):
            for px in (2 * b, 2 * b + 1):
                peer = px * 4 + after(y, k)
                dev = (zl * 4 + px, zh * 8 + after(y, k) * 2 + core)
                c = remote(wpart.at[peer], w_a.at[plane], a_s, a_r, dev)
                if k == 0:
                    pl.when(px != x)(c.start)
                else:
                    c.start()

    def w_to_line():
        w_a[plane] = wpart[plane]
        got(w_a.at[0:15], a_r)
        total = jnp.sum(w_a[...].astype(F32), axis=0)
        for p in range(4):
            w_b_src[p] = total[:, p * 128 : p * 128 + 128].astype(BF)
        for k in LINE:
            peer = lax.rem(line + k, 16)
            send(w_b_src.at[lax.rem(peer, 4)], w_b.at[line], b_s, b_r, line_peer(peer), False)
        w_b[line] = w_b_src[zl]

    def w_to_near():
        got(w_b.at[0:15], b_r)
        w_c[zl] = (jnp.sum(w_b[...].astype(F32), axis=0) * (1.0 / SHAPES)).astype(BF)
        for k in (2, 1, 15):
            send(w_c.at[zl], w_c.at[zl], c_s, c_r, line_peer(lax.rem(line + k, 16)), False)

    def w_back():
        got(w_c.at[0:3], c_r)
        for p in range(4):
            w_d[plane, :, p * 128 : p * 128 + 128] = w_c[p]
        for d in PLANE:
            send(w_d.at[plane], w_d.at[plane], d_s, d_r, plane_peer(d), False)

    def w_pair():
        got(w_d.at[0:15], d_r)
        send(w_d, dw_out.at[core], e_s, e_r, sib)
        keep(w_d, dw_out.at[core])

    def back(i):
        for b in range(2):
            backward(i, b, deltas[b])
        rs_y(i)

    for i in range(3):
        got(kv.at[:, order[i], 0:3], agy_r.at[i])
        score(i, 0)
        score(i, 1)
    for b in range(2):
        got(kv.at[b, z2, 0:3], agy_r.at[3 + b])
        score(3, b)
        combine(b)
        w_start(b)
    deltas = (delta_of(0), delta_of(1))
    for b in range(2):
        backward(3, b, deltas[b])
        rs_y_far(b)
    for i in (2, 1, 0):
        back(i)
    query_part(0)
    query_part(1)
    w_to_line()
    rs_z_far(0)
    rs_z_far(1)
    w_to_near()
    rs_z_near()
    rs_pair()
    rs_z_last(0)
    rs_z_last(1)
    w_back()
    sent(sub(zh, y, other), sib_s.at[0])
    sent(kv.at[:, 0, 0:3], agz_s)
    sent(kv.at[:, 0:3], agy_s)
    sent(dkv.at[:, 0:3], ry_s)
    sent(dqs.at[:, 0], dq_s)
    sent(w_a.at[0:15], a_s)
    sent(w_b.at[0:15], b_s)
    sent(w_c.at[0:3], c_s)
    rs_got()
    w_pair()
    last = sends.pop()
    rs_end()
    for c in sends:
        c.wait_send()
    sent(own.at[0], fin_s)
    sent(w_d.at[0:15], d_s)
    got(dw_out.at[other], e_r)
    last.wait_send()
    for c in kept:
        c.wait()


def finish(dq, dk, dv, dw, dq_out, dk_out, dv_out, dw_out, vq, vk, vv, half, full, sem):
    rest = ((dq, vq, dq_out), (dk, vk, dk_out), (dv, vv, dv_out))
    loads = [pltpu.make_async_copy(dw.at[pl.ds(i * 128, 128)], half.at[i], sem.at[i]) for i in range(4)]
    loads += [pltpu.make_async_copy(src, mid, sem.at[4 + i]) for i, (src, mid, _) in enumerate(rest)]
    stores = [pltpu.make_async_copy(full.at[i], dw_out.at[pl.ds(i * 128, 128)], sem.at[7 + i]) for i in range(4)]
    stores += [pltpu.make_async_copy(mid, dst, sem.at[11 + i]) for i, (_, mid, dst) in enumerate(rest)]
    for c in loads:
        c.start()
    for i in range(7):
        loads[i].wait()
        if i < 4:
            full[i] = half[i].astype(F32)
        stores[i].start()
    for c in stores:
        c.wait()


def shards(queries, keys, values, out_weight, out_grad):
    dma = pltpu.SemaphoreType.DMA
    vm = pltpu.VMEM
    one = pl.BlockSpec(memory_space=pltpu.HBM)
    sizes = ((ROWS, D), (LAT, D), (LAT, D))
    dq, dk, dv, dw = pl.pallas_call(
        kernel,
        out_shape=[jax.ShapeDtypeStruct(i, F32) for i in sizes] + [jax.ShapeDtypeStruct((2, 16, 16, D), BF)],
        in_specs=[one] * 5,
        out_specs=[one] * 4,
        scratch_shapes=[
            vm((2, 4, 4, 2, 2, LAT, 128), BF),
            vm((256, 256), BF),
            vm((256, D), BF),
            vm((ROWS, D), F32),
            vm((256, D), BF),
            vm((256, 256), BF),
            vm((256, 256), BF),
            vm((2, 4, 256, 512), F32),
            vm((2, 4, 128, 256), F32),
            vm((2, 1024, 512), BF),
            vm((256, 256), BF),
            vm((2, 128, 512), BF),
            vm((2, 128, 512), BF),
            vm((2, 512, 128), BF),
            vm((2, 512, 128), BF),
            vm((2, 4, 4, 2, 2, LAT, 128), BF),
            vm((4, 4, 2, 2, 2, LAT, 128), BF),
            vm((2, 1, 2, 2, LAT, 128), BF),
            vm((2, 2, 2, 2, LAT, 128), BF),
            vm((2, 2, 2, LAT, 128), BF),
            vm((2, 4, 2, 2, LAT, 128), BF),
            vm((2, LAT, D), F32),
            vm((2, 2, 128, 128), F32),
            vm((16, 16, D), BF),
            vm((16, 16, D), BF),
            vm((4, 16, 128), BF),
            vm((16, 16, 128), BF),
            vm((4, 16, 128), BF),
            vm((16, 16, D), BF),
            dma((11,)), dma((3,)), dma((3,)),
            dma, dma((10,)), dma, dma((5,)),
            dma, dma((5,)), dma((2, 5)), dma((2, 2)), dma((2,)),
            dma, dma, dma, dma,
            dma, dma, dma, dma, dma, dma, dma, dma, dma, dma,
        ],
        compiler_params=pltpu.CompilerParams(
            collective_id=0, has_side_effects=True, vmem_limit_bytes=58 * 1024 * 1024
        ),
        name="attend_back",
    )(queries[0], keys[0], values[0], out_weight, out_grad[0])
    dq, dk, dv, dw = pl.pallas_call(
        finish,
        out_shape=[jax.ShapeDtypeStruct(i, F32) for i in sizes + ((D, D),)],
        in_specs=[one] * 4,
        out_specs=[one] * 4,
        scratch_shapes=[vm(i, F32) for i in sizes] + [vm((4, 128, D), BF), vm((4, 128, D), F32), dma((14,))],
        compiler_params=pltpu.CompilerParams(vmem_limit_bytes=58 * 1024 * 1024),
        name="finish",
    )(dq, dk, dv, dw.reshape(D, D))
    return (dq[None], dk[None], dv[None], dw)


def solution(mesh):
    part = P("shape", "query", None)
    return jax.shard_map(
        shards,
        mesh=mesh,
        in_specs=(part, part, part, P(), part),
        out_specs=(part, part, part, P()),
        check_vma=False,
    )
```
